128 devices in a mesh: item: 128 (over y, x, z, core).
Axes of the slice: x: 4, y: 4, z: 4, core: 2. Of those that a mesh axis runs over, the one named last changes fastest.
Arguments:
- target_sums: float32 [64, 1572864], P(None, 'item'), may hold values from -700 to 700
- counts: int32 [1572864], P('item'), may hold values from 1 to 30
- band_offsets: int32 [12288, 4], P('item'), may hold values from -48 to 48
- band_weights: bfloat16 [12288, 4, 128, 128], P('item'), may hold values from 0 to 0.0625
- send_tiles: int32 [128, 128], P('item'), may hold values from 0 to 95
- landing_tiles: int32 [128, 128], P('item'), may hold values from 0 to 95
- remote_weights: bfloat16 [16384, 128, 128], P('item'), may hold values from 0 to 0.0625
Outputs:
- encoding: float32 [64, 1572864], P(None, 'item')
The draws below stay inside these ranges and needn't reach their ends.
All inputs are finite; a program needn't handle non-finite values.
Results may differ from the reference program's by a relative error of at most 0.0003.
Values may be sent and summed in bfloat16 or wider, within the bound.
No kernel may reach another device: no remote copies, remote signals or barrier semaphores. Data moves between devices by JAX's collectives and lax.ppermute only.
A program may use at most 128 MiB of HBM per device.

```python
import math
import jax
import jax.numpy as jnp
from jax import lax

C = 64
TILE = 128
BAND = 4
ROUNDS = 2
TILES_DEV = 96
HALF = 48
SHARDS = 128
NTILES = 12288
ITEMS = 1572864


def draw_counts(key, part):
    key = jax.random.fold_in(key, 11)
    shard = jnp.arange(ITEMS, dtype=jnp.int32) // (TILES_DEV * TILE)
    ceiling = 10 + 20 * shard // max(SHARDS - 1, 1)
    return jax.random.randint(key, (ITEMS,), 1, ceiling + 1, dtype=jnp.int32)


def draw_target_sums(key, part):
    key = jax.random.fold_in(key, 12)
    first = jax.random.fold_in(key, 0)
    second = jax.random.fold_in(key, 1)
    third = jax.random.fold_in(key, 2)
    fourth = jax.random.fold_in(key, 3)
    sixth = jax.random.fold_in(key, 5)
    shard_index = jnp.arange(ITEMS, dtype=jnp.int32) // (TILES_DEV * TILE)
    shard = shard_index.astype(jnp.float32)
    level = 6.0 * (1.0 + 2.0 * shard / max(SHARDS - 1, 1))
    flip = (1 - 2 * (shard_index % 2)).astype(jnp.float32)
    column_mean = jax.random.uniform(first, (C, 1), jnp.float32, -1.0, 1.0)
    contrast = jax.random.uniform(sixth, (C, 1), jnp.float32, 0.5, 1.0)
    row_scale = jnp.exp(jax.random.uniform(second, (1, ITEMS), jnp.float32, 0.0, math.log(10.0)))
    column_scale = jnp.exp(jax.random.uniform(fourth, (C, 1), jnp.float32, 0.0, math.log(3.0)))
    noise = jnp.clip(jax.random.normal(third, (C, ITEMS), jnp.float32), -4.0, 4.0)
    return level[None, :] * (column_mean + contrast * flip[None, :] + 0.25 * row_scale * column_scale * noise)


def draw_band_weights(key, part):
    key = jax.random.fold_in(key, 13)
    shard_index = jnp.arange(NTILES, dtype=jnp.int32) // TILES_DEV
    parity = (shard_index % 2).astype(jnp.float32)
    ceiling = (8.0 - 6.0 * parity) / TILE
    base = jax.random.uniform(key, (NTILES, BAND, TILE, TILE), jnp.float32, 0.0, 1.0)
    return (base * ceiling[:, None, None, None]).astype(jnp.bfloat16)


def draw_remote_weights(key, part):
    key = jax.random.fold_in(key, 14)
    shard_index = jnp.arange(SHARDS * SHARDS, dtype=jnp.int32) // SHARDS
    parity = (shard_index % 2).astype(jnp.float32)
    ceiling = (8.0 - 6.0 * parity) / TILE
    base = jax.random.uniform(key, (SHARDS * SHARDS, TILE, TILE), jnp.float32, 0.0, 1.0)
    return (base * ceiling[:, None, None]).astype(jnp.bfloat16)


def set_ends(values, stream_key, least, largest):
    longest = values.shape.index(max(values.shape))
    spots = []
    for shift in (0, 1):
        where = [jax.random.randint(jax.random.fold_in(stream_key, axis), (), 0, length) for axis, length in enumerate(values.shape)]
        where[longest] = (where[longest] + shift) % values.shape[longest]
        spots.append(tuple(where))
    return values.at[spots[0]].set(least).at[spots[1]].set(largest)


def setup_inputs(seed: int = 0) -> dict:
    key_of = jax.random.split(jax.random.key(seed), 8)
    return {
        "target_sums": draw_target_sums(jax.random.fold_in(key_of[7], 71), 0),
        "counts": draw_counts(jax.random.fold_in(key_of[7], 71), 0),
        "band_offsets": set_ends(jax.random.randint(key_of[2], (NTILES, BAND), -HALF, HALF + 1), jax.random.fold_in(key_of[2], 1), -HALF, HALF).astype(jnp.int32),
        "band_weights": draw_band_weights(jax.random.fold_in(key_of[7], 71), 0),
        "send_tiles": set_ends(jax.random.randint(key_of[4], (SHARDS, SHARDS), 0, TILES_DEV), jax.random.fold_in(key_of[4], 1), 0, TILES_DEV - 1).astype(jnp.int32),
        "landing_tiles": set_ends(jax.random.randint(key_of[5], (SHARDS, SHARDS), 0, TILES_DEV), jax.random.fold_in(key_of[5], 1), 0, TILES_DEV - 1).astype(jnp.int32),
        "remote_weights": draw_remote_weights(jax.random.fold_in(key_of[7], 71), 0),
    }


prior_strength = 20.0


def encode(totals, weight, mean):
    return (totals + prior_strength * mean[:, None]) / (weight[None, :] + prior_strength)


def propagate(state, band_offsets, band_weights, send_tiles, landing_tiles, remote_weights):
    channels = state.shape[0]
    tiled = state.reshape(channels, NTILES, TILE)
    padded = jnp.pad(tiled, ((0, 0), (HALF, HALF), (0, 0)))
    source_global = jnp.arange(SHARDS, dtype=jnp.int32)[None, :] * TILES_DEV + jnp.transpose(send_tiles).astype(jnp.int32)

    def shard_term(shard):
        start = (shard * TILES_DEV).astype(jnp.int32)
        window = lax.dynamic_slice_in_dim(padded, start, TILES_DEV + 2 * HALF, 1)
        offsets = lax.dynamic_slice_in_dim(band_offsets, start, TILES_DEV, 0)
        weights = lax.dynamic_slice_in_dim(band_weights, start, TILES_DEV, 0)
        position = (offsets + jnp.arange(TILES_DEV, dtype=jnp.int32)[:, None] + HALF).astype(jnp.int32)
        gathered = jnp.take(window, position, axis=1)
        summed = jnp.einsum("cdbt,dbut->cdu", gathered.astype(jnp.float32), weights.astype(jnp.float32))
        sources = jnp.take(tiled, source_global[shard], axis=1)
        remote = lax.dynamic_slice_in_dim(remote_weights, (shard * SHARDS).astype(jnp.int32), SHARDS, 0)
        partial_terms = jnp.einsum("cpt,put->cpu", sources.astype(jnp.float32), remote.astype(jnp.float32))
        landing = (landing_tiles[shard][:, None] == jnp.arange(TILES_DEV, dtype=jnp.int32)[None, :]).astype(jnp.float32)
        return summed + jnp.einsum("cpu,pd->cdu", partial_terms, landing, precision=lax.Precision.HIGHEST)

    stacked = lax.map(shard_term, jnp.arange(SHARDS, dtype=jnp.int32))
    return jnp.transpose(stacked, (1, 0, 2, 3)).reshape(channels, ITEMS)


def reference(target_sums, counts, band_offsets, band_weights, send_tiles, landing_tiles, remote_weights):
    counts_float = counts.astype(jnp.float32)
    band_rows = jnp.sum(band_weights, axis=(1, 3), dtype=jnp.float32)
    remote_rows = jnp.sum(remote_weights, axis=2, dtype=jnp.float32)
    landing_global = (jnp.arange(SHARDS, dtype=jnp.int32)[:, None] * TILES_DEV + landing_tiles.astype(jnp.int32)).reshape(-1)
    degree = band_rows.at[landing_global].add(remote_rows).reshape(-1)
    weight = counts_float + degree
    first_mean = jnp.sum(target_sums, axis=1) / jnp.sum(counts_float)
    state = encode(target_sums, counts_float, first_mean).astype(jnp.bfloat16)
    result = None
    for round_number in range(ROUNDS):
        mixed = propagate(state, band_offsets, band_weights, send_tiles, landing_tiles, remote_weights)
        totals = target_sums + mixed
        mean = jnp.sum(totals, axis=1) / jnp.sum(weight)
        result = encode(totals, weight, mean)
        state = result.astype(jnp.bfloat16)
    return result
```

```python
import functools

import jax
import jax.numpy as jnp
from jax import lax
from jax.experimental import pallas as pl
from jax.experimental.pallas import tpu as pltpu
from jax.sharding import PartitionSpec as P

PRIOR = 20.0
EXTRA = 8
F32 = jnp.float32
BF16 = jnp.bfloat16


def pieces(value, count):
    parts = []
    for _ in range(count):
        part = value.astype(BF16).astype(F32)
        parts.append(part)
        value = value - part
    return parts


def rows8(rows, base=None):
    width = 128
    index = lax.broadcasted_iota(jnp.int32, (EXTRA, width), 0)
    block = jnp.zeros((EXTRA, width), F32) if base is None else base
    for place, row in rows.items():
        block = jnp.where(index == place, row, block)
    return block


def to_row(column, shift=0):
    channels = column.shape[0]
    lane = lax.broadcasted_iota(jnp.int32, (channels, 128), 1)
    sub = lax.broadcasted_iota(jnp.int32, (channels, 128), 0)
    return jnp.sum(jnp.where(lane == sub + shift, column, 0.0), axis=0, keepdims=True)


def to_column(row, channels, shift=0):
    lane = lax.broadcasted_iota(jnp.int32, (channels, 128), 1)
    sub = lax.broadcasted_iota(jnp.int32, (channels, 128), 0)
    return jnp.sum(jnp.where(lane == sub + shift, row, 0.0), axis=1, keepdims=True)


def at_lane(scalar, place):
    lane = lax.broadcasted_iota(jnp.int32, (1, 128), 1)
    return jnp.where(lane == place, scalar, 0.0)


def pick_lane(row, place):
    lane = lax.broadcasted_iota(jnp.int32, (1, 128), 1)
    return jnp.sum(jnp.where(lane == place, row, 0.0), axis=1, keepdims=True)


def total(block):
    return jnp.sum(jnp.sum(block, axis=0, keepdims=True), axis=1, keepdims=True)


def stacked(top, bottom):
    return jnp.concatenate([top, bottom], axis=0).astype(BF16)


def product(tile, weights):
    return lax.dot_general(tile, weights, (((1,), (1,)), ((), ())), preferred_element_type=F32)


def fill_messages(send_ref, tiles_ref, out_ref, block, column_rows=None):
    count, rows, width = out_ref.shape
    top = jnp.zeros((rows - EXTRA, width), F32)
    if column_rows is None:
        shared = stacked(top, block)

    def step(q, carry):
        if column_rows is None:
            extra = shared
        else:
            high, low = pieces(column_rows[pl.ds(q, 1), :], 2)
            extra = stacked(top, rows8({6: high, 7: low}, block))
        out_ref[q] = tiles_ref[send_ref[q]] + extra
        return carry

    lax.fori_loop(0, count, step, 0, unroll=8)


def prep_kernel(send_ref, ts_ref, counts_ref, remote_ref, low_ref, high_ref, out_ref, tiles, columns, sums):
    step, steps = pl.program_id(0), pl.num_programs(0)
    channels = ts_ref.shape[0]
    here = low_ref.shape[0]
    group = remote_ref.shape[0]

    @pl.when(step == 0)
    def _():
        sums[...] = jnp.zeros_like(sums)

    for k in range(group):
        columns[pl.ds(step * group + k, 1), :] = jnp.sum(
            remote_ref[k].astype(F32), axis=0, keepdims=True
        )
    part = sums[...]
    for k in range(here):
        t = step * here + k
        block = ts_ref[:, k * 128 : (k + 1) * 128]
        count = counts_ref[pl.ds(t, 1), :].astype(F32)
        recip = 1.0 / (count + PRIOR)
        high, low = pieces(recip, 2)
        value = stacked(block * recip, rows8({0: high, 1: low, 2: jnp.ones_like(recip)}))
        tiles[t] = value

        @pl.when(step < steps // 2)
        def _():
            low_ref[k] = value

        @pl.when(step >= steps // 2)
        def _():
            high_ref[k] = value

        part = part + block
    sums[...] = part

    @pl.when(step == steps - 1)
    def _():
        row = to_row(jnp.sum(sums[...], axis=1, keepdims=True))
        row = row + at_lane(total(counts_ref[...].astype(F32)), channels)
        one, two, three = pieces(row, 3)
        fill_messages(send_ref, tiles, out_ref, rows8({3: one, 4: two, 5: three}), columns)


def column_kernel(offsets_ref, weights_ref, sums_ref):
    step = pl.program_id(0)
    here, band = weights_ref.shape[0], weights_ref.shape[1]
    reach = (sums_ref.shape[0] - pl.num_programs(0) * here) // 2

    @pl.when(step == 0)
    def _():
        sums_ref[...] = jnp.zeros_like(sums_ref)

    for k in range(here):
        t = step * here + k
        for b in range(band):
            at = t + offsets_ref[t * band + b] + reach
            row = jnp.sum(weights_ref[k, b].astype(F32), axis=0, keepdims=True)
            sums_ref[pl.ds(at, 1), :] += row


def band_kernel(with_ones, offsets_ref, below_ref, low_ref, high_ref, above_ref, weights_ref, out_ref, window):
    step = pl.program_id(0)
    here, band = weights_ref.shape[0], weights_ref.shape[1]
    reach, rows, width = below_ref.shape
    half = low_ref.shape[0]

    @pl.when(step == 0)
    def _():
        sub = lax.broadcasted_iota(jnp.int32, (rows, width), 0)
        begin = 0
        for ref in (below_ref, low_ref, high_ref, above_ref):

            def copy(k, carry, ref=ref, begin=begin):
                value = ref[k]
                if with_ones:
                    value = jnp.where(sub == rows - EXTRA + 2, 1.0, value.astype(F32)).astype(BF16)
                window[begin + k] = value
                return carry

            lax.fori_loop(0, ref.shape[0], copy, 0, unroll=4)
            begin += ref.shape[0]

    for k in range(here):
        t = step * here + k
        sources = [window[t + offsets_ref[t * band + b] + reach] for b in range(band)]
        matrices = [weights_ref[k, b] for b in range(band)]
        out_ref[k] = product(
            jnp.concatenate(sources, axis=1), jnp.concatenate(matrices, axis=1)
        )


def add_remote(landing_ref, in_ref, weights_ref, acc, seen):
    step = pl.program_id(0)
    group, rows, width = in_ref.shape

    @pl.when(step == 0)
    def _():
        acc[...] = jnp.zeros_like(acc)
        seen[...] = jnp.zeros_like(seen)

    gathered = seen[...]
    for k in range(group):
        value = in_ref[k]
        gathered = gathered + value.astype(F32)[rows - EXTRA :]
        acc[landing_ref[step * group + k]] += product(value, weights_ref[k])
    seen[...] = gathered


def copies(pairs, sems):
    return [pltpu.make_async_copy(a, b, sems.at[i]) for i, (a, b) in enumerate(pairs)]


def first_kernel(
    send_ref, landing_ref, in_ref, weights_ref, band_ref, ts_ref, counts_ref, mine_ref, from_below_ref,
    from_above_ref, low_ref, high_ref, out_ref, recip_ref, first_ref, acc, seen, band, ts, tiles, columns, sems,
):
    step, steps = pl.program_id(0), pl.num_programs(0)
    group, rows, width = in_ref.shape
    channels = rows - EXTRA
    count_tiles = counts_ref.shape[0]
    half = low_ref.shape[0]
    reach = (mine_ref.shape[0] - count_tiles) // 2

    @pl.when(step == 0)
    def _():
        for copy in copies(((band_ref, band), (ts_ref, ts)), sems):
            copy.start()
        columns[...] = mine_ref[reach : reach + count_tiles, :]
        columns[0:reach, :] += from_below_ref[...]
        columns[count_tiles - reach :, :] += from_above_ref[...]

    add_remote(landing_ref, in_ref, weights_ref, acc, seen)
    for k in range(group):
        tail = in_ref[k].astype(F32)[channels:]
        columns[pl.ds(send_ref[step * group + k], 1), :] += tail[6:7] + tail[7:8]

    @pl.when(step == steps - 1)
    def _():
        for copy in copies(((band_ref, band), (ts_ref, ts)), sems):
            copy.wait()
        known = seen[3:4, :] + seen[4:5, :] + seen[5:6, :]
        count_total = pick_lane(known, channels)
        first = PRIOR * to_column(known, channels) / count_total
        first_ref[...] = jnp.broadcast_to(known, first_ref.shape)
        zero = jnp.zeros((channels, width), F32)
        line = jnp.zeros((1, width), F32)
        carry = (zero, zero, line, line)
        for begin, ref in ((0, low_ref), (half, high_ref)):

            def finish(k, carry, begin=begin, ref=ref):
                t = begin + k
                all_totals, all_states, all_weights, all_recips = carry
                mixed = acc[t] + band[t]
                spread = mixed[channels : channels + 1] + mixed[channels + 1 : channels + 2]
                at = pl.ds(pl.multiple_of(t * width, width), width)
                totals = ts[:, at] + mixed[:channels] + first * spread
                weight = counts_ref[pl.ds(t, 1), :].astype(F32) + mixed[channels + 2 : channels + 3]
                recip = 1.0 / (weight + PRIOR)
                recip_ref[pl.ds(t, 1), :] = recip
                high, low = pieces(recip, 2)
                state = (totals * recip).astype(BF16).astype(F32)
                value = stacked(state, rows8({0: high, 1: low}))
                ref[k] = value
                tiles[t] = value
                column = columns[pl.ds(t, 1), :]
                return (
                    all_totals + totals,
                    all_states + state * column,
                    all_weights + weight,
                    all_recips + (high + low) * column,
                )

            carry = lax.fori_loop(0, half, finish, carry, unroll=4)
        all_totals, all_states, all_weights, all_recips = carry
        row = to_row(jnp.sum(all_totals, axis=1, keepdims=True))
        row = row + to_row(jnp.sum(all_states, axis=1, keepdims=True), channels)
        scalars = at_lane(total(all_weights), 0) + at_lane(total(all_recips), 1)
        one, two, three = pieces(row, 3)
        uno, due, tre = pieces(scalars, 3)
        fill_messages(
            send_ref, tiles, out_ref, rows8({2: uno, 3: one, 4: two, 5: three, 6: due, 7: tre})
        )


def last_kernel(
    landing_ref, in_ref, weights_ref, band_ref, ts_ref, recip_ref, first_ref, out_ref, acc, seen, band, ts, sems
):
    step, steps = pl.program_id(0), pl.num_programs(0)
    group, rows, width = in_ref.shape
    channels = rows - EXTRA
    count_tiles = recip_ref.shape[0]

    @pl.when(step == 0)
    def _():
        for copy in copies(((band_ref, band), (ts_ref, ts)), sems):
            copy.start()

    add_remote(landing_ref, in_ref, weights_ref, acc, seen)

    @pl.when(step == steps - 1)
    def _():
        for copy in copies(((band_ref, band), (ts_ref, ts)), sems):
            copy.wait()
        known = seen[3:4, :] + seen[4:5, :] + seen[5:6, :]
        scalars = seen[2:3, :] + seen[6:7, :] + seen[7:8, :]
        weight_total, spread_total = pick_lane(scalars, 0), pick_lane(scalars, 1)
        mean = PRIOR * to_column(known, channels) / weight_total
        mixed_total = to_column(known, channels, channels) + mean * spread_total
        last = PRIOR * (to_column(first_ref[0:1, :], channels) + mixed_total) / weight_total

        def finish(t, carry):
            mixed = acc[t] + band[t]
            spread = mixed[channels : channels + 1] + mixed[channels + 1 : channels + 2]
            at = pl.ds(pl.multiple_of(t * width, width), width)
            totals = ts[:, at] + mixed[:channels] + mean * spread
            out_ref[:, at] = (totals + last) * recip_ref[pl.ds(t, 1), :]
            return carry

        lax.fori_loop(0, count_tiles, finish, 0, unroll=4)


def params(mib):
    return pltpu.CompilerParams(vmem_limit_bytes=mib * 2**20)


def cost(flops, size):
    return pl.CostEstimate(flops=flops, bytes_accessed=size, transcendentals=0)


def whole(shape):
    zeros = (0,) * len(shape)
    return pl.BlockSpec(shape, lambda *_: zeros)


ANY = pl.BlockSpec(memory_space=pl.ANY)


def on_device(target_sums, counts, band_offsets, band_weights, send_tiles, landing_tiles, remote_weights):
    channels, columns = target_sums.shape
    count_tiles, band, width, _ = band_weights.shape
    shards = remote_weights.shape[0]
    rows = channels + EXTRA
    reach = count_tiles // 2
    half = count_tiles // 2
    counts = counts.reshape(count_tiles, width)
    send, landing, offsets = send_tiles.reshape(-1), landing_tiles.reshape(-1), band_offsets.reshape(-1)
    steps = 8
    here, group = count_tiles // steps, shards // steps
    tile_shape = jax.ShapeDtypeStruct((half, rows, width), BF16)
    message_shape = jax.ShapeDtypeStruct((shards, rows, width), BF16)
    up = [(i, i + 1) for i in range(shards - 1)]
    down = [(i + 1, i) for i in range(shards - 1)]
    sums_shape = (count_tiles + 2 * reach, width)

    low, high, outgoing = pl.pallas_call(
        prep_kernel,
        grid_spec=pltpu.PrefetchScalarGridSpec(
            num_scalar_prefetch=1,
            grid=(steps,),
            in_specs=[
                pl.BlockSpec((channels, here * width), lambda i, *_: (0, i)),
                whole((count_tiles, width)),
                pl.BlockSpec((group, width, width), lambda i, *_: (i, 0, 0)),
            ],
            out_specs=[
                pl.BlockSpec((here, rows, width), lambda i, *_: (jnp.minimum(i, steps // 2 - 1), 0, 0)),
                pl.BlockSpec((here, rows, width), lambda i, *_: (jnp.maximum(i - steps // 2, 0), 0, 0)),
                whole((shards, rows, width)),
            ],
            scratch_shapes=[
                pltpu.VMEM((count_tiles, rows, width), BF16),
                pltpu.VMEM((shards, width), F32),
                pltpu.VMEM((channels, width), F32),
            ],
        ),
        out_shape=[tile_shape, tile_shape, message_shape],
        compiler_params=params(24),
        cost_estimate=cost(10**6, 12 * 10**6),
        name="prep",
    )(send, target_sums, counts, remote_weights)

    def exchange(low, high, outgoing):
        below = lax.ppermute(high, "item", up)
        above = lax.ppermute(low, "item", down)
        incoming = lax.all_to_all(outgoing, "item", split_axis=0, concat_axis=0, tiled=True)
        return below, above, incoming

    band_steps = 12
    band_here = count_tiles // band_steps

    def band_product(with_ones, below, low, high, above):
        return pl.pallas_call(
            functools.partial(band_kernel, with_ones),
            grid_spec=pltpu.PrefetchScalarGridSpec(
                num_scalar_prefetch=1,
                grid=(band_steps,),
                in_specs=[whole((half, rows, width))] * 4
                + [pl.BlockSpec((band_here, band, width, width), lambda i, *_: (i, 0, 0, 0))],
                out_specs=pl.BlockSpec((band_here, rows, width), lambda i, *_: (i, 0, 0)),
                scratch_shapes=[pltpu.VMEM((count_tiles + 2 * reach, rows, width), BF16)],
            ),
            out_shape=jax.ShapeDtypeStruct((count_tiles, rows, width), F32),
            compiler_params=params(24),
            cost_estimate=cost(2 * 384 * 72 * 128 * 128, 20 * 10**6),
            name="band",
        )(offsets, below, low, high, above, band_weights)

    below, above, incoming = exchange(low, high, outgoing)

    column_sums = pl.pallas_call(
        column_kernel,
        grid_spec=pltpu.PrefetchScalarGridSpec(
            num_scalar_prefetch=1,
            grid=(band_steps,),
            in_specs=[pl.BlockSpec((band_here, band, width, width), lambda i, *_: (i, 0, 0, 0))],
            out_specs=whole(sums_shape),
        ),
        out_shape=jax.ShapeDtypeStruct(sums_shape, F32),
        compiler_params=params(16),
        cost_estimate=cost(10**6, 13 * 10**6),
        name="column",
    )(offsets, band_weights)
    from_below = lax.ppermute(column_sums[reach + count_tiles :], "item", up)
    from_above = lax.ppermute(column_sums[:reach], "item", down)

    mixed = band_product(True, below, low, high, above)

    remote_specs = [
        pl.BlockSpec((group, rows, width), lambda i, *_: (i, 0, 0)),
        pl.BlockSpec((group, width, width), lambda i, *_: (i, 0, 0)),
    ]
    common_scratch = [
        pltpu.VMEM((count_tiles, rows, width), F32),
        pltpu.VMEM((EXTRA, width), F32),
        pltpu.VMEM((count_tiles, rows, width), F32),
        pltpu.VMEM((channels, columns), F32),
    ]
    low, high, outgoing, recip, first = pl.pallas_call(
        first_kernel,
        grid_spec=pltpu.PrefetchScalarGridSpec(
            num_scalar_prefetch=2,
            grid=(steps,),
            in_specs=remote_specs
            + [
                ANY,
                ANY,
                whole((count_tiles, width)),
                whole(sums_shape),
                whole((reach, width)),
                whole((reach, width)),
            ],
            out_specs=[
                whole((half, rows, width)),
                whole((half, rows, width)),
                whole((shards, rows, width)),
                whole((count_tiles, width)),
                whole((8, width)),
            ],
            scratch_shapes=common_scratch
            + [
                pltpu.VMEM((count_tiles, rows, width), BF16),
                pltpu.VMEM((count_tiles, width), F32),
                pltpu.SemaphoreType.DMA((2,)),
            ],
        ),
        out_shape=[
            tile_shape,
            tile_shape,
            message_shape,
            jax.ShapeDtypeStruct((count_tiles, width), F32),
            jax.ShapeDtypeStruct((8, width), F32),
        ],
        compiler_params=params(40),
        cost_estimate=cost(2 * 128 * 72 * 128 * 128, 20 * 10**6),
        name="first",
    )(send, landing, incoming, remote_weights, mixed, target_sums, counts, column_sums, from_below, from_above)

    below, above, incoming = exchange(low, high, outgoing)
    mixed = band_product(False, below, low, high, above)
    return pl.pallas_call(
        last_kernel,
        grid_spec=pltpu.PrefetchScalarGridSpec(
            num_scalar_prefetch=1,
            grid=(steps,),
            in_specs=remote_specs + [ANY, ANY, whole((count_tiles, width)), whole((8, width))],
            out_specs=whole((channels, columns)),
            scratch_shapes=common_scratch + [pltpu.SemaphoreType.DMA((2,))],
        ),
        out_shape=jax.ShapeDtypeStruct((channels, columns), F32),
        compiler_params=params(40),
        cost_estimate=cost(2 * 128 * 72 * 128 * 128, 20 * 10**6),
        name="last",
    )(landing, incoming, remote_weights, mixed, target_sums, recip, first)


def solution(mesh):
    return jax.shard_map(
        on_device,
        mesh=mesh,
        in_specs=(
            P(None, "item"),
            P("item"),
            P("item", None),
            P("item", None, None, None),
            P("item", None),
            P("item", None),
            P("item", None, None),
        ),
        out_specs=P(None, "item"),
        check_vma=False,
    )
```

```python
import functools

import jax
import jax.numpy as jnp
from jax import lax
from jax.experimental import pallas as pl
from jax.experimental.pallas import tpu as pltpu
from jax.sharding import PartitionSpec as P

PRIOR = 20.0
EXTRA = 8
F32 = jnp.float32
BF16 = jnp.bfloat16
LOADS = 8
BAND_LOADS = 12
PARTS = 4
BAND_COST = 10**11
VMEM = 60
VMEM_ROUND = 60
VMEM_BAND = 52
AHEAD = 3


def pieces(value, count):
    parts = []
    for _ in range(count):
        part = value.astype(BF16).astype(F32)
        parts.append(part)
        value = value - part
    return parts


def rows8(rows, base=None):
    width = 128
    index = lax.broadcasted_iota(jnp.int32, (EXTRA, width), 0)
    block = jnp.zeros((EXTRA, width), F32) if base is None else base
    for place, row in rows.items():
        block = jnp.where(index == place, row, block)
    return block


def to_row(column, shift=0):
    channels = column.shape[0]
    lane = lax.broadcasted_iota(jnp.int32, (channels, 128), 1)
    sub = lax.broadcasted_iota(jnp.int32, (channels, 128), 0)
    return jnp.sum(jnp.where(lane == sub + shift, column, 0.0), axis=0, keepdims=True)


def to_column(row, channels, shift=0):
    lane = lax.broadcasted_iota(jnp.int32, (channels, 128), 1)
    sub = lax.broadcasted_iota(jnp.int32, (channels, 128), 0)
    return jnp.sum(jnp.where(lane == sub + shift, row, 0.0), axis=1, keepdims=True)


def at_lane(scalar, place):
    lane = lax.broadcasted_iota(jnp.int32, (1, 128), 1)
    return jnp.where(lane == place, scalar, 0.0)


def pick_lane(row, place):
    lane = lax.broadcasted_iota(jnp.int32, (1, 128), 1)
    return jnp.sum(jnp.where(lane == place, row, 0.0), axis=1, keepdims=True)


def total(block):
    return jnp.sum(jnp.sum(block, axis=0, keepdims=True), axis=1, keepdims=True)


def stacked(top, bottom):
    return jnp.concatenate([top, bottom], axis=0).astype(BF16)


def product(tile, weights):
    return lax.dot_general(tile, weights, (((1,), (1,)), ((), ())), preferred_element_type=F32)


class Loads:
    def __init__(self, pairs, count, sems, first):
        self.parts, self.count = [], count
        for i in range(count):
            part = []
            for number, (source, target, axis) in enumerate(pairs):
                size = source.shape[axis] // count
                at = (slice(None),) * axis + (pl.ds(i * size, size),)
                sem = sems.at[first + i * len(pairs) + number]
                part.append(pltpu.make_async_copy(source.at[at], target.at[at], sem))
            self.parts.append(part)

    def start(self, i):
        if i < self.count:
            for copy in self.parts[i]:
                copy.start()

    def wait(self, i):
        for copy in self.parts[i]:
            copy.wait()


def send_messages(send_ref, tiles, messages, out_ref, sems, first_sem, block, column_rows=None):
    count, rows, width = messages.shape
    top = jnp.zeros((rows - EXTRA, width), F32)
    if column_rows is None:
        shared = stacked(top, block)
    stores = []
    part = count // PARTS
    for number in range(PARTS):

        def step(k, carry, number=number):
            q = number * part + k
            if column_rows is None:
                extra = shared
            else:
                high, low = pieces(column_rows[pl.ds(q, 1), :], 2)
                extra = stacked(top, rows8({6: high, 7: low}, block))
            messages[q] = tiles[send_ref[q]] + extra
            return carry

        lax.fori_loop(0, part, step, 0, unroll=8)
        at = pl.ds(number * part, part)
        stores.append(
            pltpu.make_async_copy(messages.at[at], out_ref.at[at], sems.at[first_sem + number])
        )
        stores[-1].start()
    return stores


def prep_kernel(
    send_ref, ts_ref, counts_ref, remote_ref, low_ref, high_ref, out_ref,
    ts, remote, tiles, messages, columns, sems, out_sems,
):
    channels, width = ts.shape[0], columns.shape[1]
    count_tiles, shards = tiles.shape[0], messages.shape[0]
    half = count_tiles // 2
    here, group = count_tiles // LOADS, shards // LOADS
    ts_loads = Loads([(ts_ref, ts, 1)], LOADS, sems, 0)
    remote_loads = Loads([(remote_ref, remote, 0)], LOADS, sems, LOADS)
    loads = [(ts_loads, i) for i in range(LOADS)] + [(remote_loads, i) for i in range(LOADS)]
    for group_loads, i in loads[: 2 * AHEAD]:
        group_loads.start(i)

    def start_next(done):
        for group_loads, i in loads[done + 2 * AHEAD : done + 2 * AHEAD + 1]:
            group_loads.start(i)

    stores = [
        pltpu.make_async_copy(tiles.at[pl.ds(0, half)], low_ref, out_sems.at[0]),
        pltpu.make_async_copy(tiles.at[pl.ds(half, half)], high_ref, out_sems.at[1]),
    ]
    part = jnp.zeros((channels, width), F32)
    for load in range(LOADS):
        ts_loads.wait(load)
        start_next(load)

        def tile(k, part, load=load):
            t = load * here + k
            block = ts[:, pl.ds(pl.multiple_of(t * width, width), width)]
            count = counts_ref[pl.ds(t, 1), :].astype(F32)
            recip = 1.0 / (count + PRIOR)
            high, low = pieces(recip, 2)
            tiles[t] = stacked(block * recip, rows8({0: high, 1: low, 2: jnp.ones_like(recip)}))
            return part + block

        part = lax.fori_loop(0, here, tile, part, unroll=4)
        if load == LOADS // 2 - 1:
            stores[0].start()
    stores[1].start()
    for load in range(LOADS):
        remote_loads.wait(load)
        start_next(LOADS + load)

        def column(k, carry, load=load):
            p = load * group + k
            columns[pl.ds(p, 1), :] = jnp.sum(remote[p].astype(F32), axis=0, keepdims=True)
            return carry

        lax.fori_loop(0, group, column, 0, unroll=4)
    row = to_row(jnp.sum(part, axis=1, keepdims=True))
    row = row + at_lane(total(counts_ref[...].astype(F32)), channels)
    one, two, three = pieces(row, 3)
    block = rows8({3: one, 4: two, 5: three})
    stores += send_messages(send_ref, tiles, messages, out_ref, out_sems, 2, block, columns)
    for store in stores:
        store.wait()


def band_kernel(
    with_ones, offsets_ref, ts_ref, counts_ref, below_ref, low_ref, high_ref, above_ref, weights_ref, out_ref, *rest
):
    if with_ones:
        sums_ref, ts, weights, window, result, sems, out_sems = rest
    else:
        ts, weights, window, result, sems, out_sems = rest
    count_tiles, band = weights.shape[:2]
    reach, rows, width = below_ref.shape
    channels = rows - EXTRA
    here = count_tiles // BAND_LOADS
    parts = []
    for i, ref in enumerate((below_ref, low_ref, high_ref, above_ref)):
        parts.append(pltpu.make_async_copy(ref, window.at[pl.ds(i * reach, reach)], sems.at[2 * BAND_LOADS + i]))
        parts[-1].start()
    loads = Loads([(weights_ref, weights, 0), (ts_ref, ts, 1)], BAND_LOADS, sems, 0)
    for load in range(AHEAD):
        loads.start(load)
    if with_ones:
        sums_ref[...] = jnp.zeros_like(sums_ref)
    for copy in parts:
        copy.wait()
    if with_ones:
        sub = lax.broadcasted_iota(jnp.int32, (rows, width), 0)
        for begin in (0, reach + count_tiles):

            def fix(k, carry, begin=begin):
                value = window[begin + k].astype(F32)
                window[begin + k] = jnp.where(sub == channels + 2, 1.0, value).astype(BF16)
                return carry

            lax.fori_loop(0, reach, fix, 0, unroll=4)
    stores = Loads([(result, out_ref, 0)], BAND_LOADS, out_sems, 0)
    for load in range(BAND_LOADS):
        loads.start(load + AHEAD)
        loads.wait(load)

        def tile(k, carry, load=load):
            t = load * here + k
            places = [t + offsets_ref[t * band + b] + reach for b in range(band)]
            matrices = [weights[t, b] for b in range(band)]
            sources = jnp.concatenate([window[place] for place in places], axis=1)
            mixed = product(sources, jnp.concatenate(matrices, axis=1))
            known = [ts[:, pl.ds(pl.multiple_of(t * width, width), width)]]
            known.append(rows8({2: counts_ref[pl.ds(t, 1), :].astype(F32)}))
            result[t] = mixed + jnp.concatenate(known, axis=0)
            if with_ones:
                for place, matrix in zip(places, matrices):
                    sums_ref[pl.ds(place, 1), :] += jnp.sum(matrix.astype(F32), axis=0, keepdims=True)
            return carry

        lax.fori_loop(0, here, tile, 0, unroll=4)
        stores.start(load)
    for load in range(BAND_LOADS):
        stores.wait(load)


def add_remote(landing_ref, in_ref, weights_ref, band_ref, incoming, weights, band, acc, sems, each=None):
    shards, rows, width = incoming.shape
    group = shards // LOADS
    loads = Loads([(in_ref, incoming, 0), (weights_ref, weights, 0)], LOADS, sems, 0)
    band_loads = Loads([(band_ref, band, 0)], PARTS, sems, 2 * LOADS)
    for load in range(AHEAD):
        loads.start(load)

    def clear(t, carry):
        acc[t] = jnp.zeros((rows, width), F32)
        return carry

    lax.fori_loop(0, acc.shape[0], clear, 0, unroll=8)
    seen = jnp.zeros((EXTRA, width), F32)
    for load in range(LOADS):
        loads.start(load + AHEAD)
        if load + AHEAD >= LOADS:
            band_loads.start(load + AHEAD - LOADS)
        loads.wait(load)

        def tile(k, seen, load=load):
            p = load * group + k
            value = incoming[p]
            tail = value.astype(F32)[rows - EXTRA :]
            acc[landing_ref[p]] += product(value, weights[p])
            if each is not None:
                each(p, tail)
            return seen + tail

        seen = lax.fori_loop(0, group, tile, seen, unroll=16)
    for part in range(AHEAD, PARTS):
        band_loads.start(part)
    return seen, band_loads


def first_kernel(
    send_ref, landing_ref, in_ref, weights_ref, band_ref, columns_ref,
    low_ref, high_ref, out_ref, recip_ref, first_ref,
    incoming, weights, band, acc, tiles, messages, columns, recips, firsts, sems, out_sems,
):
    shards, rows, width = incoming.shape
    channels = rows - EXTRA
    count_tiles = acc.shape[0]
    half = count_tiles // 2
    column_load = pltpu.make_async_copy(columns_ref, columns, out_sems.at[0])
    column_load.start()
    column_load.wait()

    def each(p, tail):
        columns[pl.ds(send_ref[p], 1), :] += tail[6:7] + tail[7:8]

    seen, band_loads = add_remote(
        landing_ref, in_ref, weights_ref, band_ref, incoming, weights, band, acc, sems, each
    )
    known = seen[3:4, :] + seen[4:5, :] + seen[5:6, :]
    count_total = pick_lane(known, channels)
    first = jnp.broadcast_to(PRIOR * to_column(known, channels) / count_total, (channels, width))
    firsts[...] = jnp.broadcast_to(known, firsts.shape)
    zero = jnp.zeros((channels, width), F32)
    line = jnp.zeros((1, width), F32)
    carry = (zero, zero, line, line)
    stores = []
    part = count_tiles // PARTS
    for number in range(PARTS):
        band_loads.wait(number)

        def finish(k, carry, number=number):
            t = number * part + k
            all_totals, all_states, all_weights, all_recips = carry
            mixed = acc[t] + band[t]
            spread = mixed[channels : channels + 1] + mixed[channels + 1 : channels + 2]
            totals = mixed[:channels] + first * spread
            weight = mixed[channels + 2 : channels + 3]
            recip = 1.0 / (weight + PRIOR)
            recips[pl.ds(t, 1), :] = recip
            high, low = pieces(recip, 2)
            state = (totals * recip).astype(BF16).astype(F32)
            tiles[t] = stacked(state, rows8({0: high, 1: low}))
            column = columns[pl.ds(t, 1), :]
            return (
                all_totals + totals,
                all_states + state * column,
                all_weights + weight,
                all_recips + (high + low) * column,
            )

        carry = lax.fori_loop(0, part, finish, carry, unroll=4)
        ref = low_ref if number < PARTS // 2 else high_ref
        at = pl.ds(number * part % half, part)
        stores.append(
            pltpu.make_async_copy(tiles.at[pl.ds(number * part, part)], ref.at[at], out_sems.at[number])
        )
        stores[-1].start()
    for source, ref in ((recips, recip_ref), (firsts, first_ref)):
        stores.append(pltpu.make_async_copy(source, ref, out_sems.at[len(stores)]))
        stores[-1].start()
    all_totals, all_states, all_weights, all_recips = carry
    row = to_row(jnp.sum(all_totals, axis=1, keepdims=True))
    row = row + to_row(jnp.sum(all_states, axis=1, keepdims=True), channels)
    scalars = at_lane(total(all_weights), 0) + at_lane(total(all_recips), 1)
    one, two, three = pieces(row, 3)
    uno, due, tre = pieces(scalars, 3)
    block = rows8({2: uno, 3: one, 4: two, 5: three, 6: due, 7: tre})
    stores += send_messages(send_ref, tiles, messages, out_ref, out_sems, len(stores), block)
    for store in stores:
        store.wait()


def last_kernel(
    landing_ref, in_ref, weights_ref, band_ref, recip_ref, first_ref, out_ref,
    incoming, weights, band, acc, result, recips, firsts, sems, out_sems,
):
    shards, rows, width = incoming.shape
    channels = rows - EXTRA
    count_tiles = acc.shape[0]
    small = [
        pltpu.make_async_copy(recip_ref, recips, out_sems.at[0]),
        pltpu.make_async_copy(first_ref, firsts, out_sems.at[1]),
    ]
    for load in small:
        load.start()
    seen, band_loads = add_remote(
        landing_ref, in_ref, weights_ref, band_ref, incoming, weights, band, acc, sems
    )
    for load in small:
        load.wait()
    known = seen[3:4, :] + seen[4:5, :] + seen[5:6, :]
    scalars = seen[2:3, :] + seen[6:7, :] + seen[7:8, :]
    weight_total, spread_total = pick_lane(scalars, 0), pick_lane(scalars, 1)
    mean = PRIOR * to_column(known, channels) / weight_total
    mixed_total = to_column(known, channels, channels) + mean * spread_total
    last = PRIOR * (to_column(firsts[0:1, :], channels) + mixed_total) / weight_total
    mean, last = jnp.broadcast_to(mean, (channels, width)), jnp.broadcast_to(last, (channels, width))
    stores = []
    part = count_tiles // PARTS
    for number in range(PARTS):
        band_loads.wait(number)

        def finish(k, carry, number=number):
            t = number * part + k
            mixed = acc[t] + band[t]
            spread = mixed[channels : channels + 1] + mixed[channels + 1 : channels + 2]
            at = pl.ds(pl.multiple_of(t * width, width), width)
            result[:, at] = (mixed[:channels] + mean * spread + last) * recips[pl.ds(t, 1), :]
            return carry

        lax.fori_loop(0, part, finish, 0, unroll=4)
        at = pl.ds(number * part * width, part * width)
        stores.append(pltpu.make_async_copy(result.at[:, at], out_ref.at[:, at], out_sems.at[number]))
        stores[-1].start()
    for store in stores:
        store.wait()


def params(mib):
    return pltpu.CompilerParams(vmem_limit_bytes=mib * 2**20)


def cost(flops, size):
    return pl.CostEstimate(flops=flops, bytes_accessed=size, transcendentals=0)


def whole(shape):
    zeros = (0,) * len(shape)
    return pl.BlockSpec(shape, lambda *_: zeros)


ANY = pl.BlockSpec(memory_space=pl.ANY)


def shapes(count_tiles, rows, shards, width=128):
    tile = jax.ShapeDtypeStruct((count_tiles // 2, rows, width), BF16)
    message = jax.ShapeDtypeStruct((shards, rows, width), BF16)
    return tile, message


def call(kernel, prefetch, in_specs, out_specs, out_shape, scratch, name, estimate, limit=VMEM):
    return pl.pallas_call(
        kernel,
        grid_spec=pltpu.PrefetchScalarGridSpec(
            num_scalar_prefetch=prefetch,
            grid=(1,),
            in_specs=in_specs,
            out_specs=out_specs,
            scratch_shapes=scratch,
        ),
        out_shape=out_shape,
        compiler_params=params(limit),
        cost_estimate=estimate,
        name=name,
    )


def sems(count):
    return pltpu.SemaphoreType.DMA((count,))


def prep(send, ts, counts, remote_weights):
    channels, columns = ts.shape
    count_tiles, width = counts.shape
    shards = remote_weights.shape[0]
    rows = channels + EXTRA
    tile, message = shapes(count_tiles, rows, shards)
    scratch = [
        pltpu.VMEM(ts.shape, F32),
        pltpu.VMEM(remote_weights.shape, BF16),
        pltpu.VMEM((count_tiles, rows, width), BF16),
        pltpu.VMEM(message.shape, BF16),
        pltpu.VMEM((shards, width), F32),
        sems(2 * LOADS),
        sems(2 + PARTS),
    ]
    return call(
        prep_kernel, 1, [ANY, whole(counts.shape), ANY], [ANY] * 3, [tile, tile, message], scratch, "prep",
        cost(10**6, 12 * 10**6),
    )(send, ts, counts, remote_weights)


def band_product(with_ones, offsets, ts, counts, below, low, high, above, band_weights):
    count_tiles, _, width, _ = band_weights.shape
    rows = low.shape[1]
    shape = (count_tiles, rows, width)
    scratch = [
        pltpu.VMEM(ts.shape, F32),
        pltpu.VMEM(band_weights.shape, BF16),
        pltpu.VMEM((2 * count_tiles, rows, width), BF16),
        pltpu.VMEM(shape, F32),
        sems(2 * BAND_LOADS + 4),
        sems(BAND_LOADS),
    ]
    out_shape, out_specs = [jax.ShapeDtypeStruct(shape, F32)], [ANY]
    if with_ones:
        out_shape.append(jax.ShapeDtypeStruct((2 * count_tiles, width), F32))
        out_specs.append(whole(out_shape[1].shape))
    return call(
        functools.partial(band_kernel, with_ones), 1, [ANY, whole(counts.shape)] + [ANY] * 5, out_specs,
        out_shape, scratch, "band", cost(BAND_COST, 20 * 10**6), VMEM_BAND,
    )(offsets, ts, counts, below, low, high, above, band_weights)


def round_scratch(incoming, remote_weights, mixed):
    return [
        pltpu.VMEM(incoming.shape, BF16),
        pltpu.VMEM(remote_weights.shape, BF16),
        pltpu.VMEM(mixed.shape, F32),
        pltpu.VMEM(mixed.shape, F32),
    ]


def first_round(send, landing, incoming, remote_weights, mixed, columns):
    shards, rows, width = incoming.shape
    count_tiles = mixed.shape[0]
    tile, message = shapes(count_tiles, rows, shards)
    recip = jax.ShapeDtypeStruct((count_tiles, width), F32)
    first = jax.ShapeDtypeStruct((8, width), F32)
    scratch = round_scratch(incoming, remote_weights, mixed) + [
        pltpu.VMEM(mixed.shape, BF16),
        pltpu.VMEM(incoming.shape, BF16),
        pltpu.VMEM(columns.shape, F32),
        pltpu.VMEM(recip.shape, F32),
        pltpu.VMEM(first.shape, F32),
        sems(PARTS + 2 * LOADS),
        sems(2 + 2 * PARTS),
    ]
    return call(
        first_kernel, 2, [ANY] * 4, [ANY] * 5, [tile, tile, message, recip, first], scratch, "first",
        cost(2 * 128 * 72 * 128 * 128, 20 * 10**6), VMEM_ROUND,
    )(send, landing, incoming, remote_weights, mixed, columns)


def last_round(landing, incoming, remote_weights, mixed, recip, first):
    rows, width = incoming.shape[1:]
    shape = (rows - EXTRA, mixed.shape[0] * width)
    scratch = round_scratch(incoming, remote_weights, mixed) + [
        pltpu.VMEM(shape, F32),
        pltpu.VMEM(recip.shape, F32),
        pltpu.VMEM(first.shape, F32),
        sems(PARTS + 2 * LOADS),
        sems(PARTS),
    ]
    return call(
        last_kernel, 1, [ANY] * 5, ANY, jax.ShapeDtypeStruct(shape, F32), scratch, "last",
        cost(2 * 128 * 72 * 128 * 128, 20 * 10**6), VMEM_ROUND,
    )(landing, incoming, remote_weights, mixed, recip, first)


def on_device(target_sums, counts, band_offsets, band_weights, send_tiles, landing_tiles, remote_weights):
    count_tiles, _, width, _ = band_weights.shape
    shards = remote_weights.shape[0]
    reach = count_tiles // 2
    counts = counts.reshape(count_tiles, width)
    send, landing, offsets = send_tiles.reshape(-1), landing_tiles.reshape(-1), band_offsets.reshape(-1)
    up = [(i, i + 1) for i in range(shards - 1)]
    down = [(i + 1, i) for i in range(shards - 1)]

    def exchange(low, high, outgoing):
        below = lax.ppermute(high, "item", up)
        above = lax.ppermute(low, "item", down)
        incoming = lax.all_to_all(outgoing, "item", split_axis=0, concat_axis=0, tiled=True)
        return below, above, incoming

    low, high, outgoing = prep(send, target_sums, counts, remote_weights)
    below, above, incoming = exchange(low, high, outgoing)
    mixed, sums = band_product(True, offsets, target_sums, counts, below, low, high, above, band_weights)
    from_below = lax.ppermute(sums[reach + count_tiles :], "item", up)
    from_above = lax.ppermute(sums[:reach], "item", down)
    columns = sums[reach : reach + count_tiles] + jnp.concatenate([from_below, from_above], axis=0)
    low, high, outgoing, recip, first = first_round(send, landing, incoming, remote_weights, mixed, columns)
    below, above, incoming = exchange(low, high, outgoing)
    (mixed,) = band_product(False, offsets, target_sums, counts, below, low, high, above, band_weights)
    return last_round(landing, incoming, remote_weights, mixed, recip, first)


def solution(mesh):
    return jax.shard_map(
        on_device,
        mesh=mesh,
        in_specs=(
            P(None, "item"),
            P("item"),
            P("item", None),
            P("item", None, None, None),
            P("item", None),
            P("item", None),
            P("item", None, None),
        ),
        out_specs=P(None, "item"),
        check_vma=False,
    )
```

```python
import functools

import jax
import jax.numpy as jnp
from jax import lax
from jax.experimental import pallas as pl
from jax.experimental.pallas import tpu as pltpu
from jax.sharding import PartitionSpec as P

PRIOR = 20.0
EXTRA = 8
F32 = jnp.float32
BF16 = jnp.bfloat16
LOADS = 8
BAND_LOADS = 12
PARTS = 4
BAND_COST = 10**11
VMEM = 60
VMEM_ROUND = 60
VMEM_BAND = 52
AHEAD = 3
GROUP = 16
SLOTS = 3


def pieces(value, count):
    parts = []
    for _ in range(count):
        part = value.astype(BF16).astype(F32)
        parts.append(part)
        value = value - part
    return parts


def rows8(rows, base=None):
    width = 128
    index = lax.broadcasted_iota(jnp.int32, (EXTRA, width), 0)
    block = jnp.zeros((EXTRA, width), F32) if base is None else base
    for place, row in rows.items():
        block = jnp.where(index == place, row, block)
    return block


def to_row(column, shift=0):
    channels = column.shape[0]
    lane = lax.broadcasted_iota(jnp.int32, (channels, 128), 1)
    sub = lax.broadcasted_iota(jnp.int32, (channels, 128), 0)
    return jnp.sum(jnp.where(lane == sub + shift, column, 0.0), axis=0, keepdims=True)


def to_column(row, channels, shift=0):
    lane = lax.broadcasted_iota(jnp.int32, (channels, 128), 1)
    sub = lax.broadcasted_iota(jnp.int32, (channels, 128), 0)
    return jnp.sum(jnp.where(lane == sub + shift, row, 0.0), axis=1, keepdims=True)


def at_lane(scalar, place):
    lane = lax.broadcasted_iota(jnp.int32, (1, 128), 1)
    return jnp.where(lane == place, scalar, 0.0)


def pick_lane(row, place):
    lane = lax.broadcasted_iota(jnp.int32, (1, 128), 1)
    return jnp.sum(jnp.where(lane == place, row, 0.0), axis=1, keepdims=True)


def total(block):
    return jnp.sum(jnp.sum(block, axis=0, keepdims=True), axis=1, keepdims=True)


def stacked(top, bottom):
    return jnp.concatenate([top, bottom], axis=0).astype(BF16)


def product(tile, weights):
    return lax.dot_general(tile, weights, (((1,), (1,)), ((), ())), preferred_element_type=F32)


class Loads:
    def __init__(self, pairs, count, sems, first):
        self.parts, self.count = [], count
        for i in range(count):
            part = []
            for number, (source, target, axis) in enumerate(pairs):
                size = source.shape[axis] // count
                at = (slice(None),) * axis + (pl.ds(i * size, size),)
                sem = sems.at[first + i * len(pairs) + number]
                part.append(pltpu.make_async_copy(source.at[at], target.at[at], sem))
            self.parts.append(part)

    def start(self, i):
        if i < self.count:
            for copy in self.parts[i]:
                copy.start()

    def wait(self, i):
        for copy in self.parts[i]:
            copy.wait()


def two_products(tiles, weights):
    rows, width = tiles[0].shape
    both = product(jnp.concatenate(tiles, axis=0), jnp.concatenate(weights, axis=0))
    return both[:rows, :width], both[rows:, width:]


def send_messages(send_ref, tiles, messages, out_ref, sems, first_sem, block, column_rows=None):
    count, rows, width = messages.shape
    top = jnp.zeros((rows - EXTRA, width), F32)
    if column_rows is None:
        shared = stacked(top, block)
    stores = []
    part = count // PARTS
    for number in range(PARTS):

        def step(k, carry, number=number):
            q = number * part + k
            if column_rows is None:
                extra = shared
            else:
                high, low = pieces(column_rows[pl.ds(q, 1), :], 2)
                extra = stacked(top, rows8({6: high, 7: low}, block))
            messages[q] = tiles[send_ref[q]] + extra
            return carry

        lax.fori_loop(0, part, step, 0, unroll=8)
        at = pl.ds(number * part, part)
        stores.append(
            pltpu.make_async_copy(messages.at[at], out_ref.at[at], sems.at[first_sem + number])
        )
        stores[-1].start()
    return stores


def prep_kernel(
    send_ref, ts_ref, counts_ref, remote_ref, low_ref, high_ref, out_ref,
    ts, remote, tiles, messages, columns, sems, out_sems,
):
    channels, width = ts.shape[0], columns.shape[1]
    count_tiles, shards = tiles.shape[0], messages.shape[0]
    half = count_tiles // 2
    here, group = count_tiles // LOADS, shards // LOADS
    ts_loads = Loads([(ts_ref, ts, 1)], LOADS, sems, 0)
    remote_loads = Loads([(remote_ref, remote, 0)], LOADS, sems, LOADS)
    loads = [(ts_loads, i) for i in range(LOADS)] + [(remote_loads, i) for i in range(LOADS)]
    for group_loads, i in loads[: 2 * AHEAD]:
        group_loads.start(i)

    def start_next(done):
        for group_loads, i in loads[done + 2 * AHEAD : done + 2 * AHEAD + 1]:
            group_loads.start(i)

    stores = [
        pltpu.make_async_copy(tiles.at[pl.ds(0, half)], low_ref, out_sems.at[0]),
        pltpu.make_async_copy(tiles.at[pl.ds(half, half)], high_ref, out_sems.at[1]),
    ]
    part = jnp.zeros((channels, width), F32)
    for load in range(LOADS):
        ts_loads.wait(load)
        start_next(load)

        def tile(k, part, load=load):
            t = load * here + k
            block = ts[:, pl.ds(pl.multiple_of(t * width, width), width)]
            count = counts_ref[pl.ds(t, 1), :].astype(F32)
            recip = 1.0 / (count + PRIOR)
            high, low = pieces(recip, 2)
            tiles[t] = stacked(block * recip, rows8({0: high, 1: low, 2: jnp.ones_like(recip)}))
            return part + block

        part = lax.fori_loop(0, here, tile, part, unroll=4)
        if load == LOADS // 2 - 1:
            stores[0].start()
    stores[1].start()
    for load in range(LOADS):
        remote_loads.wait(load)
        start_next(LOADS + load)

        def column(k, carry, load=load):
            p = load * group + k
            columns[pl.ds(p, 1), :] = jnp.sum(remote[p].astype(F32), axis=0, keepdims=True)
            return carry

        lax.fori_loop(0, group, column, 0, unroll=4)
    row = to_row(jnp.sum(part, axis=1, keepdims=True))
    row = row + at_lane(total(counts_ref[...].astype(F32)), channels)
    one, two, three = pieces(row, 3)
    block = rows8({3: one, 4: two, 5: three})
    stores += send_messages(send_ref, tiles, messages, out_ref, out_sems, 2, block, columns)
    for store in stores:
        store.wait()


def list_far_pairs(offsets_ref, far_ref, count_tiles, band, reach):
    room = far_ref.shape[0] // 4

    def pair(i, found):
        destination = i // band
        source = destination + offsets_ref[i]
        below = source < 0
        far = jnp.logical_or(below, source >= count_tiles)
        far_ref[found] = source + jnp.where(below, reach, reach - count_tiles)
        far_ref[room + found] = i
        far_ref[2 * room + found] = destination
        return found + far.astype(jnp.int32)

    found = lax.fori_loop(0, count_tiles * band, pair, 0, unroll=8)
    for i in range(GROUP):
        far_ref[found + i] = 2 * reach
        far_ref[room + found + i] = 0
        far_ref[2 * room + found + i] = 0
    far_ref[3 * room] = found


def band_kernel(with_ones, offsets_ref, ts_ref, counts_ref, low_ref, high_ref, weights_ref, out_ref, *rest):
    if with_ones:
        sums_ref, far_ref, ts, weights, window, result, sems, out_sems = rest
    else:
        ts, weights, window, result, sems, out_sems = rest
    count_tiles, band = weights.shape[:2]
    half, rows, width = low_ref.shape
    channels = rows - EXTRA
    here = count_tiles // BAND_LOADS
    parts = []
    for i, ref in enumerate((low_ref, high_ref)):
        parts.append(pltpu.make_async_copy(ref, window.at[pl.ds(i * half, half)], sems.at[2 * BAND_LOADS + i]))
        parts[-1].start()
    loads = Loads([(weights_ref, weights, 0), (ts_ref, ts, 1)], BAND_LOADS, sems, 0)
    for load in range(AHEAD):
        loads.start(load)
    sub = lax.broadcasted_iota(jnp.int32, (rows, width), 0)
    window[count_tiles] = jnp.where(sub == channels + 2, 1.0, 0.0).astype(BF16)
    if with_ones:
        sums_ref[...] = jnp.zeros_like(sums_ref)
        reach = (sums_ref.shape[0] - count_tiles) // 2
        list_far_pairs(offsets_ref, far_ref, count_tiles, band, reach)
    for copy in parts:
        copy.wait()
    stores = Loads([(result, out_ref, 0)], BAND_LOADS, out_sems, 0)
    for load in range(BAND_LOADS):
        loads.start(load + AHEAD)
        loads.wait(load)

        def tile(k, carry, load=load):
            t = load * here + k
            places = [t + offsets_ref[t * band + b] for b in range(band)]
            near = [jnp.logical_and(place >= 0, place < count_tiles) for place in places]
            sources = [window[jnp.where(n, place, count_tiles)] for n, place in zip(near, places)]
            matrices = [weights[t, b] for b in range(band)]
            mixed = product(jnp.concatenate(sources, axis=1), jnp.concatenate(matrices, axis=1))
            known = [ts[:, pl.ds(pl.multiple_of(t * width, width), width)]]
            known.append(rows8({2: counts_ref[pl.ds(t, 1), :].astype(F32)}))
            result[t] = mixed + jnp.concatenate(known, axis=0)
            if with_ones:
                for place, matrix in zip(places, matrices):
                    sums_ref[pl.ds(place + reach, 1), :] += jnp.sum(matrix.astype(F32), axis=0, keepdims=True)
            return carry

        lax.fori_loop(0, here, tile, 0, unroll=4)
        stores.start(load)
    for load in range(BAND_LOADS):
        stores.wait(load)


def add_far(landing_ref, far_ref, ins, scratch, each=None):
    in_ref, weights_ref, band_ref, below_ref, above_ref, band_weights_ref = ins
    incoming, weights, band, acc, halo, far_weights, sems, far_sems = scratch
    shards, rows, width = incoming.shape
    group = shards // LOADS
    reach = below_ref.shape[0]
    room = far_ref.shape[0] // 4
    loads = Loads([(in_ref, incoming, 0), (weights_ref, weights, 0)], LOADS, sems, 0)
    band_loads = Loads([(band_ref, band, 0)], PARTS, sems, 2 * LOADS)
    halo_loads = [
        pltpu.make_async_copy(below_ref, halo.at[pl.ds(0, reach)], sems.at[2 * LOADS + PARTS]),
        pltpu.make_async_copy(above_ref, halo.at[pl.ds(reach, reach)], sems.at[2 * LOADS + PARTS + 1]),
    ]
    for load in range(AHEAD):
        loads.start(load)
    groups = (far_ref[3 * room] + GROUP - 1) // GROUP

    def far_copies(g):
        slot = lax.rem(g, SLOTS)
        result = []
        for k in range(GROUP):
            pair = far_ref[room + g * GROUP + k]
            source = band_weights_ref.at[pair]
            result.append(
                pltpu.make_async_copy(source, far_weights.at[slot * GROUP + k], far_sems.at[slot * GROUP + k])
            )
        return result

    def start_group(g):
        @pl.when(g < groups)
        def _():
            for copy in far_copies(g):
                copy.start()

    def clear(t, carry):
        acc[t] = jnp.zeros((rows, width), F32)
        return carry

    lax.fori_loop(0, acc.shape[0], clear, 0, unroll=8)
    halo[2 * reach] = jnp.zeros((rows, width), BF16)
    seen = jnp.zeros((EXTRA, width), F32)
    for load in range(LOADS):
        loads.start(load + AHEAD)
        if load + AHEAD == LOADS:
            for copy in halo_loads:
                copy.start()
        if load + AHEAD > LOADS:
            start_group(load + AHEAD - LOADS - 1)
        loads.wait(load)

        def pair(k, seen, load=load):
            p = load * group + 2 * k
            values = [incoming[p], incoming[p + 1]]
            tails = [value.astype(F32)[rows - EXTRA :] for value in values]
            mixed = two_products(values, [weights[p], weights[p + 1]])
            for i in range(2):
                acc[landing_ref[p + i]] += mixed[i]
                if each is not None:
                    each(p + i, tails[i])
            return seen + (tails[0] + tails[1])

        seen = lax.fori_loop(0, group // 2, pair, seen, unroll=8)
    for copy in halo_loads:
        copy.wait()
    for part in range(PARTS):
        band_loads.start(part)
    for g in range(AHEAD - 1, SLOTS):
        start_group(g)
    sub = lax.broadcasted_iota(jnp.int32, (EXTRA, width), 0)

    def far_group(g, carry):
        for copy in far_copies(g):
            copy.wait()
        slot = lax.rem(g, SLOTS)
        for k in range(0, GROUP, 2):
            at = [g * GROUP + k + i for i in range(2)]
            mixed = two_products(
                [halo[far_ref[i]] for i in at], [far_weights[slot * GROUP + k + i] for i in range(2)]
            )
            for i in range(2):
                tail = jnp.where(sub == 2, 0.0, mixed[i][rows - EXTRA :])
                full = jnp.concatenate([mixed[i][: rows - EXTRA], tail], axis=0)
                acc[far_ref[2 * room + at[i]]] += full
        start_group(g + SLOTS)
        return carry

    lax.fori_loop(0, groups, far_group, 0)
    return seen, band_loads


def first_kernel(send_ref, landing_ref, far_ref, *refs):
    ins, columns_ref, (low_ref, high_ref, out_ref, recip_ref, first_ref) = refs[:6], refs[6], refs[7:12]
    scratch, (tiles, messages, columns, recips, firsts, out_sems) = refs[12:20], refs[20:]
    band, acc = scratch[2:4]
    _, rows, width = scratch[0].shape
    channels = rows - EXTRA
    count_tiles = acc.shape[0]
    half = count_tiles // 2
    column_load = pltpu.make_async_copy(columns_ref, columns, out_sems.at[0])
    column_load.start()
    column_load.wait()

    def each(p, tail):
        columns[pl.ds(send_ref[p], 1), :] += tail[6:7] + tail[7:8]

    seen, band_loads = add_far(landing_ref, far_ref, ins, scratch, each)
    known = seen[3:4, :] + seen[4:5, :] + seen[5:6, :]
    count_total = pick_lane(known, channels)
    first = jnp.broadcast_to(PRIOR * to_column(known, channels) / count_total, (channels, width))
    firsts[...] = jnp.broadcast_to(known, firsts.shape)
    zero = jnp.zeros((channels, width), F32)
    line = jnp.zeros((1, width), F32)
    carry = (zero, zero, line, line)
    stores = []
    part = count_tiles // PARTS
    for number in range(PARTS):
        band_loads.wait(number)

        def finish(k, carry, number=number):
            t = number * part + k
            all_totals, all_states, all_weights, all_recips = carry
            mixed = acc[t] + band[t]
            spread = mixed[channels : channels + 1] + mixed[channels + 1 : channels + 2]
            totals = mixed[:channels] + first * spread
            weight = mixed[channels + 2 : channels + 3]
            recip = 1.0 / (weight + PRIOR)
            recips[pl.ds(t, 1), :] = recip
            high, low = pieces(recip, 2)
            state = (totals * recip).astype(BF16).astype(F32)
            tiles[t] = stacked(state, rows8({0: high, 1: low}))
            column = columns[pl.ds(t, 1), :]
            return (
                all_totals + totals,
                all_states + state * column,
                all_weights + weight,
                all_recips + (high + low) * column,
            )

        carry = lax.fori_loop(0, part, finish, carry, unroll=4)
        ref = low_ref if number < PARTS // 2 else high_ref
        at = pl.ds(number * part % half, part)
        stores.append(
            pltpu.make_async_copy(tiles.at[pl.ds(number * part, part)], ref.at[at], out_sems.at[number])
        )
        stores[-1].start()
    for source, ref in ((recips, recip_ref), (firsts, first_ref)):
        stores.append(pltpu.make_async_copy(source, ref, out_sems.at[len(stores)]))
        stores[-1].start()
    all_totals, all_states, all_weights, all_recips = carry
    row = to_row(jnp.sum(all_totals, axis=1, keepdims=True))
    row = row + to_row(jnp.sum(all_states, axis=1, keepdims=True), channels)
    scalars = at_lane(total(all_weights), 0) + at_lane(total(all_recips), 1)
    one, two, three = pieces(row, 3)
    uno, due, tre = pieces(scalars, 3)
    block = rows8({2: uno, 3: one, 4: two, 5: three, 6: due, 7: tre})
    stores += send_messages(send_ref, tiles, messages, out_ref, out_sems, len(stores), block)
    for store in stores:
        store.wait()


def last_kernel(landing_ref, far_ref, *refs):
    ins, (recip_ref, first_ref, out_ref) = refs[:6], refs[6:9]
    scratch, (result, recips, firsts, out_sems) = refs[9:17], refs[17:]
    band, acc = scratch[2:4]
    _, rows, width = scratch[0].shape
    channels = rows - EXTRA
    count_tiles = acc.shape[0]
    small = [
        pltpu.make_async_copy(recip_ref, recips, out_sems.at[0]),
        pltpu.make_async_copy(first_ref, firsts, out_sems.at[1]),
    ]
    for load in small:
        load.start()
    seen, band_loads = add_far(landing_ref, far_ref, ins, scratch)
    for load in small:
        load.wait()
    known = seen[3:4, :] + seen[4:5, :] + seen[5:6, :]
    scalars = seen[2:3, :] + seen[6:7, :] + seen[7:8, :]
    weight_total, spread_total = pick_lane(scalars, 0), pick_lane(scalars, 1)
    mean = PRIOR * to_column(known, channels) / weight_total
    mixed_total = to_column(known, channels, channels) + mean * spread_total
    last = PRIOR * (to_column(firsts[0:1, :], channels) + mixed_total) / weight_total
    mean, last = jnp.broadcast_to(mean, (channels, width)), jnp.broadcast_to(last, (channels, width))
    stores = []
    part = count_tiles // PARTS
    for number in range(PARTS):
        band_loads.wait(number)

        def finish(k, carry, number=number):
            t = number * part + k
            mixed = acc[t] + band[t]
            spread = mixed[channels : channels + 1] + mixed[channels + 1 : channels + 2]
            at = pl.ds(pl.multiple_of(t * width, width), width)
            result[:, at] = (mixed[:channels] + mean * spread + last) * recips[pl.ds(t, 1), :]
            return carry

        lax.fori_loop(0, part, finish, 0, unroll=4)
        at = pl.ds(number * part * width, part * width)
        stores.append(pltpu.make_async_copy(result.at[:, at], out_ref.at[:, at], out_sems.at[number]))
        stores[-1].start()
    for store in stores:
        store.wait()


def params(mib):
    return pltpu.CompilerParams(vmem_limit_bytes=mib * 2**20)


def cost(flops, size):
    return pl.CostEstimate(flops=flops, bytes_accessed=size, transcendentals=0)


def whole(shape):
    zeros = (0,) * len(shape)
    return pl.BlockSpec(shape, lambda *_: zeros)


ANY = pl.BlockSpec(memory_space=pl.ANY)


def shapes(count_tiles, rows, shards, width=128):
    tile = jax.ShapeDtypeStruct((count_tiles // 2, rows, width), BF16)
    message = jax.ShapeDtypeStruct((shards, rows, width), BF16)
    return tile, message


def call(kernel, prefetch, in_specs, out_specs, out_shape, scratch, name, estimate, limit=VMEM):
    return pl.pallas_call(
        kernel,
        grid_spec=pltpu.PrefetchScalarGridSpec(
            num_scalar_prefetch=prefetch,
            grid=(1,),
            in_specs=in_specs,
            out_specs=out_specs,
            scratch_shapes=scratch,
        ),
        out_shape=out_shape,
        compiler_params=params(limit),
        cost_estimate=estimate,
        name=name,
    )


def sems(count):
    return pltpu.SemaphoreType.DMA((count,))


def prep(send, ts, counts, remote_weights):
    channels, columns = ts.shape
    count_tiles, width = counts.shape
    shards = remote_weights.shape[0]
    rows = channels + EXTRA
    tile, message = shapes(count_tiles, rows, shards)
    scratch = [
        pltpu.VMEM(ts.shape, F32),
        pltpu.VMEM(remote_weights.shape, BF16),
        pltpu.VMEM((count_tiles, rows, width), BF16),
        pltpu.VMEM(message.shape, BF16),
        pltpu.VMEM((shards, width), F32),
        sems(2 * LOADS),
        sems(2 + PARTS),
    ]
    return call(
        prep_kernel, 1, [ANY, whole(counts.shape), ANY], [ANY] * 3, [tile, tile, message], scratch, "prep",
        cost(10**6, 12 * 10**6),
    )(send, ts, counts, remote_weights)


def band_product(with_ones, offsets, ts, counts, low, high, band_weights):
    count_tiles, band, width, _ = band_weights.shape
    rows = low.shape[1]
    shape = (count_tiles, rows, width)
    scratch = [
        pltpu.VMEM(ts.shape, F32),
        pltpu.VMEM(band_weights.shape, BF16),
        pltpu.VMEM((count_tiles + 1, rows, width), BF16),
        pltpu.VMEM(shape, F32),
        sems(2 * BAND_LOADS + 2),
        sems(BAND_LOADS),
    ]
    out_shape, out_specs = [jax.ShapeDtypeStruct(shape, F32)], [ANY]
    if with_ones:
        room = -(-(count_tiles * band + GROUP + 1) // 512) * 512
        out_shape.append(jax.ShapeDtypeStruct((2 * count_tiles, width), F32))
        out_shape.append(jax.ShapeDtypeStruct((4 * room,), jnp.int32))
        out_specs += [whole(out_shape[1].shape), pl.BlockSpec(memory_space=pltpu.SMEM)]
    return call(
        functools.partial(band_kernel, with_ones), 1, [ANY, whole(counts.shape)] + [ANY] * 3, out_specs,
        out_shape, scratch, "band", cost(BAND_COST, 20 * 10**6), VMEM_BAND,
    )(offsets, ts, counts, low, high, band_weights)


def round_scratch(incoming, remote_weights, mixed, below):
    rows, width = below.shape[1:]
    return [
        pltpu.VMEM(incoming.shape, BF16),
        pltpu.VMEM(remote_weights.shape, BF16),
        pltpu.VMEM(mixed.shape, F32),
        pltpu.VMEM(mixed.shape, F32),
        pltpu.VMEM((2 * below.shape[0] + 1, rows, width), BF16),
        pltpu.VMEM((SLOTS * GROUP, width, width), BF16),
        sems(PARTS + 2 * LOADS + 2),
        sems(SLOTS * GROUP),
    ]


def first_round(send, landing, far, incoming, remote_weights, mixed, below, above, band_weights, columns):
    shards, rows, width = incoming.shape
    count_tiles = mixed.shape[0]
    tile, message = shapes(count_tiles, rows, shards)
    recip = jax.ShapeDtypeStruct((count_tiles, width), F32)
    first = jax.ShapeDtypeStruct((8, width), F32)
    scratch = round_scratch(incoming, remote_weights, mixed, below) + [
        pltpu.VMEM(mixed.shape, BF16),
        pltpu.VMEM(incoming.shape, BF16),
        pltpu.VMEM(columns.shape, F32),
        pltpu.VMEM(recip.shape, F32),
        pltpu.VMEM(first.shape, F32),
        sems(2 + 2 * PARTS),
    ]
    return call(
        first_kernel, 3, [ANY] * 7, [ANY] * 5, [tile, tile, message, recip, first], scratch, "first",
        cost(2 * 128 * 72 * 128 * 128, 20 * 10**6), VMEM_ROUND,
    )(send, landing, far, incoming, remote_weights, mixed, below, above, band_weights, columns)


def last_round(landing, far, incoming, remote_weights, mixed, below, above, band_weights, recip, first):
    rows, width = incoming.shape[1:]
    shape = (rows - EXTRA, mixed.shape[0] * width)
    scratch = round_scratch(incoming, remote_weights, mixed, below) + [
        pltpu.VMEM(shape, F32),
        pltpu.VMEM(recip.shape, F32),
        pltpu.VMEM(first.shape, F32),
        sems(PARTS),
    ]
    return call(
        last_kernel, 2, [ANY] * 8, ANY, jax.ShapeDtypeStruct(shape, F32), scratch, "last",
        cost(2 * 128 * 72 * 128 * 128, 20 * 10**6), VMEM_ROUND,
    )(landing, far, incoming, remote_weights, mixed, below, above, band_weights, recip, first)


def on_device(target_sums, counts, band_offsets, band_weights, send_tiles, landing_tiles, remote_weights):
    count_tiles, _, width, _ = band_weights.shape
    shards = remote_weights.shape[0]
    reach = count_tiles // 2
    counts = counts.reshape(count_tiles, width)
    send, landing, offsets = send_tiles.reshape(-1), landing_tiles.reshape(-1), band_offsets.reshape(-1)
    flat_weights = band_weights.reshape(-1, width, width)
    up = [(i, i + 1) for i in range(shards - 1)]
    down = [(i + 1, i) for i in range(shards - 1)]

    def exchange(low, high, outgoing):
        below = lax.ppermute(high, "item", up)
        above = lax.ppermute(low, "item", down)
        incoming = lax.all_to_all(outgoing, "item", split_axis=0, concat_axis=0, tiled=True)
        return below, above, incoming

    low, high, outgoing = prep(send, target_sums, counts, remote_weights)
    below, above, incoming = exchange(low, high, outgoing)
    mixed, sums, far = band_product(True, offsets, target_sums, counts, low, high, band_weights)
    from_below = lax.ppermute(sums[reach + count_tiles :], "item", up)
    from_above = lax.ppermute(sums[:reach], "item", down)
    columns = sums[reach : reach + count_tiles] + jnp.concatenate([from_below, from_above], axis=0)
    low, high, outgoing, recip, first = first_round(
        send, landing, far, incoming, remote_weights, mixed, below, above, flat_weights, columns
    )
    below, above, incoming = exchange(low, high, outgoing)
    (mixed,) = band_product(False, offsets, target_sums, counts, low, high, band_weights)
    return last_round(
        landing, far, incoming, remote_weights, mixed, below, above, flat_weights, recip, first
    )


def solution(mesh):
    return jax.shard_map(
        on_device,
        mesh=mesh,
        in_specs=(
            P(None, "item"),
            P("item"),
            P("item", None),
            P("item", None, None, None),
            P("item", None),
            P("item", None),
            P("item", None, None),
        ),
        out_specs=P(None, "item"),
        check_vma=False,
    )
```

```python
import functools

import jax
import jax.numpy as jnp
from jax import lax
from jax.experimental import pallas as pl
from jax.experimental.pallas import tpu as pltpu
from jax.sharding import PartitionSpec as P

PRIOR = 20.0
EXTRA = 8
F32 = jnp.float32
BF16 = jnp.bfloat16
LOADS = 8
BAND_LOADS = 12
PARTS = 4
BAND_COST = 10**11
MESSAGE_COST = 10**6
VMEM = 60
VMEM_ROUND = 60
VMEM_BAND = 52
AHEAD = 3


def pieces(value, count):
    parts = []
    for _ in range(count):
        part = value.astype(BF16).astype(F32)
        parts.append(part)
        value = value - part
    return parts


def rows8(rows, base=None):
    width = 128
    index = lax.broadcasted_iota(jnp.int32, (EXTRA, width), 0)
    block = jnp.zeros((EXTRA, width), F32) if base is None else base
    for place, row in rows.items():
        block = jnp.where(index == place, row, block)
    return block


def to_row(column, shift=0):
    channels = column.shape[0]
    lane = lax.broadcasted_iota(jnp.int32, (channels, 128), 1)
    sub = lax.broadcasted_iota(jnp.int32, (channels, 128), 0)
    return jnp.sum(jnp.where(lane == sub + shift, column, 0.0), axis=0, keepdims=True)


def to_column(row, channels, shift=0):
    lane = lax.broadcasted_iota(jnp.int32, (channels, 128), 1)
    sub = lax.broadcasted_iota(jnp.int32, (channels, 128), 0)
    return jnp.sum(jnp.where(lane == sub + shift, row, 0.0), axis=1, keepdims=True)


def at_lane(scalar, place):
    lane = lax.broadcasted_iota(jnp.int32, (1, 128), 1)
    return jnp.where(lane == place, scalar, 0.0)


def pick_lane(row, place):
    lane = lax.broadcasted_iota(jnp.int32, (1, 128), 1)
    return jnp.sum(jnp.where(lane == place, row, 0.0), axis=1, keepdims=True)


def total(block):
    return jnp.sum(jnp.sum(block, axis=0, keepdims=True), axis=1, keepdims=True)


def stacked(top, bottom):
    return jnp.concatenate([top, bottom], axis=0).astype(BF16)


def product(tile, weights):
    return lax.dot_general(tile, weights, (((1,), (1,)), ((), ())), preferred_element_type=F32)


class Loads:
    def __init__(self, pairs, count, sems, first):
        self.parts, self.count = [], count
        for i in range(count):
            part = []
            for number, (source, target, axis) in enumerate(pairs):
                size = source.shape[axis] // count
                at = (slice(None),) * axis + (pl.ds(i * size, size),)
                sem = sems.at[first + i * len(pairs) + number]
                part.append(pltpu.make_async_copy(source.at[at], target.at[at], sem))
            self.parts.append(part)

    def start(self, i):
        if i < self.count:
            for copy in self.parts[i]:
                copy.start()

    def wait(self, i):
        for copy in self.parts[i]:
            copy.wait()


def two_products(tiles, weights):
    rows, width = tiles[0].shape
    both = product(jnp.concatenate(tiles, axis=0), jnp.concatenate(weights, axis=0))
    return both[:rows, :width], both[rows:, width:]


def message_kernel(with_columns, send_ref, low_ref, high_ref, block_ref, *rest):
    if with_columns:
        remote_ref, out_ref, tiles, messages, block, sems, out_sems, remote, columns = rest
    else:
        out_ref, tiles, messages, block, sems, out_sems = rest
    count, rows, width = messages.shape
    half = low_ref.shape[0]
    loads = [
        pltpu.make_async_copy(low_ref, tiles.at[pl.ds(0, half)], sems.at[0]),
        pltpu.make_async_copy(high_ref, tiles.at[pl.ds(half, half)], sems.at[1]),
        pltpu.make_async_copy(block_ref, block, sems.at[2]),
    ]
    for load in loads:
        load.start()
    top = jnp.zeros((rows - EXTRA, width), F32)
    part = count // PARTS
    if with_columns:
        remote_loads = Loads([(remote_ref, remote, 0)], PARTS, sems, 3)
        for i in range(PARTS):
            remote_loads.start(i)
    for load in loads:
        load.wait()
    shared = block[...]
    stores = Loads([(messages, out_ref, 0)], PARTS, out_sems, 0)
    for number in range(PARTS):
        if with_columns:
            remote_loads.wait(number)

            def column(k, carry, number=number):
                q = number * part + k
                columns[pl.ds(q, 1), :] = jnp.sum(remote[q].astype(F32), axis=0, keepdims=True)
                return carry

            lax.fori_loop(0, part, column, 0, unroll=8)

        def step(k, carry, number=number):
            q = number * part + k
            extra = shared
            if with_columns:
                high, low = pieces(columns[pl.ds(q, 1), :], 2)
                extra = rows8({6: high, 7: low}, shared)
            messages[q] = tiles[send_ref[q]] + stacked(top, extra)
            return carry

        lax.fori_loop(0, part, step, 0, unroll=8)
        stores.start(number)
    for number in range(PARTS):
        stores.wait(number)


def prep_kernel(ts_ref, counts_ref, low_ref, high_ref, block_ref, ts, tiles, sems, out_sems):
    channels, width = ts.shape[0], counts_ref.shape[1]
    count_tiles = tiles.shape[0]
    half = count_tiles // 2
    here = count_tiles // LOADS
    loads = Loads([(ts_ref, ts, 1)], LOADS, sems, 0)
    for load in range(2 * AHEAD):
        loads.start(load)
    stores = [
        pltpu.make_async_copy(tiles.at[pl.ds(0, half)], low_ref, out_sems.at[0]),
        pltpu.make_async_copy(tiles.at[pl.ds(half, half)], high_ref, out_sems.at[1]),
    ]
    part = jnp.zeros((channels, width), F32)
    for load in range(LOADS):
        loads.wait(load)
        loads.start(load + 2 * AHEAD)

        def tile(k, part, load=load):
            t = load * here + k
            block = ts[:, pl.ds(pl.multiple_of(t * width, width), width)]
            count = counts_ref[pl.ds(t, 1), :].astype(F32)
            recip = 1.0 / (count + PRIOR)
            high, low = pieces(recip, 2)
            tiles[t] = stacked(block * recip, rows8({0: high, 1: low, 2: jnp.ones_like(recip)}))
            return part + block

        part = lax.fori_loop(0, here, tile, part, unroll=4)
        if load == LOADS // 2 - 1:
            stores[0].start()
    stores[1].start()
    row = to_row(jnp.sum(part, axis=1, keepdims=True))
    row = row + at_lane(total(counts_ref[...].astype(F32)), channels)
    one, two, three = pieces(row, 3)
    block_ref[...] = rows8({3: one, 4: two, 5: three})
    for store in stores:
        store.wait()


def band_kernel(
    with_ones, offsets_ref, ts_ref, counts_ref, below_ref, low_ref, high_ref, above_ref, weights_ref, out_ref, *rest
):
    if with_ones:
        sums_ref, ts, weights, window, result, sems, out_sems = rest
    else:
        ts, weights, window, result, sems, out_sems = rest
    count_tiles, band = weights.shape[:2]
    reach, rows, width = below_ref.shape
    channels = rows - EXTRA
    here = count_tiles // BAND_LOADS
    parts = []
    for i, ref in enumerate((below_ref, low_ref, high_ref, above_ref)):
        parts.append(pltpu.make_async_copy(ref, window.at[pl.ds(i * reach, reach)], sems.at[2 * BAND_LOADS + i]))
        parts[-1].start()
    loads = Loads([(weights_ref, weights, 0), (ts_ref, ts, 1)], BAND_LOADS, sems, 0)
    for load in range(AHEAD):
        loads.start(load)
    if with_ones:
        sums_ref[...] = jnp.zeros_like(sums_ref)
    for copy in parts:
        copy.wait()
    if with_ones:
        sub = lax.broadcasted_iota(jnp.int32, (rows, width), 0)
        for begin in (0, reach + count_tiles):

            def fix(k, carry, begin=begin):
                value = window[begin + k].astype(F32)
                window[begin + k] = jnp.where(sub == channels + 2, 1.0, value).astype(BF16)
                return carry

            lax.fori_loop(0, reach, fix, 0, unroll=4)
    stores = Loads([(result, out_ref, 0)], BAND_LOADS, out_sems, 0)
    for load in range(BAND_LOADS):
        loads.start(load + AHEAD)
        loads.wait(load)

        def tile(k, carry, load=load):
            t = load * here + k
            places = [t + offsets_ref[t * band + b] + reach for b in range(band)]
            matrices = [weights[t, b] for b in range(band)]
            sources = jnp.concatenate([window[place] for place in places], axis=1)
            mixed = product(sources, jnp.concatenate(matrices, axis=1))
            known = [ts[:, pl.ds(pl.multiple_of(t * width, width), width)]]
            known.append(rows8({2: counts_ref[pl.ds(t, 1), :].astype(F32)}))
            result[t] = mixed + jnp.concatenate(known, axis=0)
            if with_ones:
                for place, matrix in zip(places, matrices):
                    sums_ref[pl.ds(place, 1), :] += jnp.sum(matrix.astype(F32), axis=0, keepdims=True)
            return carry

        lax.fori_loop(0, here, tile, 0, unroll=4)
        stores.start(load)
    for load in range(BAND_LOADS):
        stores.wait(load)


def add_remote(landing_ref, in_ref, weights_ref, band_ref, incoming, weights, band, acc, sems, each=None):
    shards, rows, width = incoming.shape
    group = shards // LOADS
    loads = Loads([(in_ref, incoming, 0), (weights_ref, weights, 0)], LOADS, sems, 0)
    band_loads = Loads([(band_ref, band, 0)], PARTS, sems, 2 * LOADS)
    for load in range(AHEAD):
        loads.start(load)

    def clear(t, carry):
        acc[t] = jnp.zeros((rows, width), F32)
        return carry

    lax.fori_loop(0, acc.shape[0], clear, 0, unroll=8)
    seen = jnp.zeros((EXTRA, width), F32)
    for load in range(LOADS):
        loads.start(load + AHEAD)
        if load + AHEAD >= LOADS:
            band_loads.start(load + AHEAD - LOADS)
        loads.wait(load)

        def pair(k, seen, load=load):
            p = load * group + 2 * k
            values = [incoming[p], incoming[p + 1]]
            tails = [value.astype(F32)[rows - EXTRA :] for value in values]
            mixed = two_products(values, [weights[p], weights[p + 1]])
            for i in range(2):
                acc[landing_ref[p + i]] += mixed[i]
                if each is not None:
                    each(p + i, tails[i])
            return seen + (tails[0] + tails[1])

        seen = lax.fori_loop(0, group // 2, pair, seen, unroll=8)
    for part in range(AHEAD, PARTS):
        band_loads.start(part)
    return seen, band_loads


def first_kernel(
    send_ref, landing_ref, in_ref, weights_ref, band_ref, columns_ref,
    low_ref, high_ref, block_ref, recip_ref, first_ref,
    incoming, weights, band, acc, tiles, columns, recips, firsts, block, sems, out_sems,
):
    shards, rows, width = incoming.shape
    channels = rows - EXTRA
    count_tiles = acc.shape[0]
    half = count_tiles // 2
    column_load = pltpu.make_async_copy(columns_ref, columns, out_sems.at[0])
    column_load.start()
    column_load.wait()

    def each(p, tail):
        columns[pl.ds(send_ref[p], 1), :] += tail[6:7] + tail[7:8]

    seen, band_loads = add_remote(
        landing_ref, in_ref, weights_ref, band_ref, incoming, weights, band, acc, sems, each
    )
    known = seen[3:4, :] + seen[4:5, :] + seen[5:6, :]
    count_total = pick_lane(known, channels)
    first = jnp.broadcast_to(PRIOR * to_column(known, channels) / count_total, (channels, width))
    firsts[...] = jnp.broadcast_to(known, firsts.shape)
    zero = jnp.zeros((channels, width), F32)
    line = jnp.zeros((1, width), F32)
    carry = (zero, zero, line, line)
    stores = []
    part = count_tiles // PARTS
    for number in range(PARTS):
        band_loads.wait(number)

        def finish(k, carry, number=number):
            t = number * part + k
            all_totals, all_states, all_weights, all_recips = carry
            mixed = acc[t] + band[t]
            spread = mixed[channels : channels + 1] + mixed[channels + 1 : channels + 2]
            totals = mixed[:channels] + first * spread
            weight = mixed[channels + 2 : channels + 3]
            recip = 1.0 / (weight + PRIOR)
            recips[pl.ds(t, 1), :] = recip
            high, low = pieces(recip, 2)
            state = (totals * recip).astype(BF16).astype(F32)
            tiles[t] = stacked(state, rows8({0: high, 1: low}))
            column = columns[pl.ds(t, 1), :]
            return (
                all_totals + totals,
                all_states + state * column,
                all_weights + weight,
                all_recips + (high + low) * column,
            )

        carry = lax.fori_loop(0, part, finish, carry, unroll=4)
        ref = low_ref if number < PARTS // 2 else high_ref
        at = pl.ds(number * part % half, part)
        stores.append(
            pltpu.make_async_copy(tiles.at[pl.ds(number * part, part)], ref.at[at], out_sems.at[number])
        )
        stores[-1].start()
    all_totals, all_states, all_weights, all_recips = carry
    row = to_row(jnp.sum(all_totals, axis=1, keepdims=True))
    row = row + to_row(jnp.sum(all_states, axis=1, keepdims=True), channels)
    scalars = at_lane(total(all_weights), 0) + at_lane(total(all_recips), 1)
    one, two, three = pieces(row, 3)
    uno, due, tre = pieces(scalars, 3)
    block[...] = rows8({2: uno, 3: one, 4: two, 5: three, 6: due, 7: tre})
    for source, ref in ((recips, recip_ref), (firsts, first_ref), (block, block_ref)):
        stores.append(pltpu.make_async_copy(source, ref, out_sems.at[len(stores)]))
        stores[-1].start()
    for store in stores:
        store.wait()


def last_kernel(
    landing_ref, in_ref, weights_ref, band_ref, recip_ref, first_ref, out_ref,
    incoming, weights, band, acc, result, recips, firsts, sems, out_sems,
):
    shards, rows, width = incoming.shape
    channels = rows - EXTRA
    count_tiles = acc.shape[0]
    small = [
        pltpu.make_async_copy(recip_ref, recips, out_sems.at[0]),
        pltpu.make_async_copy(first_ref, firsts, out_sems.at[1]),
    ]
    for load in small:
        load.start()
    seen, band_loads = add_remote(
        landing_ref, in_ref, weights_ref, band_ref, incoming, weights, band, acc, sems
    )
    for load in small:
        load.wait()
    known = seen[3:4, :] + seen[4:5, :] + seen[5:6, :]
    scalars = seen[2:3, :] + seen[6:7, :] + seen[7:8, :]
    weight_total, spread_total = pick_lane(scalars, 0), pick_lane(scalars, 1)
    mean = PRIOR * to_column(known, channels) / weight_total
    mixed_total = to_column(known, channels, channels) + mean * spread_total
    last = PRIOR * (to_column(firsts[0:1, :], channels) + mixed_total) / weight_total
    mean, last = jnp.broadcast_to(mean, (channels, width)), jnp.broadcast_to(last, (channels, width))
    stores = []
    part = count_tiles // PARTS
    for number in range(PARTS):
        band_loads.wait(number)

        def finish(k, carry, number=number):
            t = number * part + k
            mixed = acc[t] + band[t]
            spread = mixed[channels : channels + 1] + mixed[channels + 1 : channels + 2]
            at = pl.ds(pl.multiple_of(t * width, width), width)
            result[:, at] = (mixed[:channels] + mean * spread + last) * recips[pl.ds(t, 1), :]
            return carry

        lax.fori_loop(0, part, finish, 0, unroll=4)
        at = pl.ds(number * part * width, part * width)
        stores.append(pltpu.make_async_copy(result.at[:, at], out_ref.at[:, at], out_sems.at[number]))
        stores[-1].start()
    for store in stores:
        store.wait()


def params(mib):
    return pltpu.CompilerParams(vmem_limit_bytes=mib * 2**20)


def cost(flops, size):
    return pl.CostEstimate(flops=flops, bytes_accessed=size, transcendentals=0)


def whole(shape):
    zeros = (0,) * len(shape)
    return pl.BlockSpec(shape, lambda *_: zeros)


ANY = pl.BlockSpec(memory_space=pl.ANY)


def shapes(count_tiles, rows, shards, width=128):
    tile = jax.ShapeDtypeStruct((count_tiles // 2, rows, width), BF16)
    message = jax.ShapeDtypeStruct((shards, rows, width), BF16)
    return tile, message


def call(kernel, prefetch, in_specs, out_specs, out_shape, scratch, name, estimate, limit=VMEM):
    return pl.pallas_call(
        kernel,
        grid_spec=pltpu.PrefetchScalarGridSpec(
            num_scalar_prefetch=prefetch,
            grid=(1,),
            in_specs=in_specs,
            out_specs=out_specs,
            scratch_shapes=scratch,
        ),
        out_shape=out_shape,
        compiler_params=params(limit),
        cost_estimate=estimate,
        name=name,
    )


def sems(count):
    return pltpu.SemaphoreType.DMA((count,))


def prep(ts, counts, shards):
    channels, columns = ts.shape
    count_tiles, width = counts.shape
    rows = channels + EXTRA
    tile, _ = shapes(count_tiles, rows, shards)
    scratch = [pltpu.VMEM(ts.shape, F32), pltpu.VMEM((count_tiles, rows, width), BF16), sems(LOADS), sems(2)]
    block = jax.ShapeDtypeStruct((EXTRA, width), F32)
    return call(
        prep_kernel, 0, [ANY, whole(counts.shape)], [ANY, ANY, whole(block.shape)], [tile, tile, block], scratch,
        "prep", cost(10**6, 5 * 10**6),
    )(ts, counts)


def fill_messages(send, low, high, block, remote_weights=None):
    half, rows, width = low.shape
    shards = send.shape[0]
    _, message = shapes(2 * half, rows, shards)
    scratch = [
        pltpu.VMEM((2 * half, rows, width), BF16),
        pltpu.VMEM(message.shape, BF16),
        pltpu.VMEM(block.shape, F32),
        sems(3 + PARTS),
        sems(PARTS),
    ]
    operands = [send, low, high, block]
    if remote_weights is not None:
        operands.append(remote_weights)
        scratch += [pltpu.VMEM(remote_weights.shape, BF16), pltpu.VMEM((shards, width), F32)]
    return call(
        functools.partial(message_kernel, remote_weights is not None), 1, [ANY] * (len(operands) - 1), ANY,
        message, scratch, "messages", cost(MESSAGE_COST, 5 * 10**6),
    )(*operands)


def band_product(with_ones, offsets, ts, counts, below, low, high, above, band_weights):
    count_tiles, _, width, _ = band_weights.shape
    rows = low.shape[1]
    shape = (count_tiles, rows, width)
    scratch = [
        pltpu.VMEM(ts.shape, F32),
        pltpu.VMEM(band_weights.shape, BF16),
        pltpu.VMEM((2 * count_tiles, rows, width), BF16),
        pltpu.VMEM(shape, F32),
        sems(2 * BAND_LOADS + 4),
        sems(BAND_LOADS),
    ]
    out_shape, out_specs = [jax.ShapeDtypeStruct(shape, F32)], [ANY]
    if with_ones:
        out_shape.append(jax.ShapeDtypeStruct((2 * count_tiles, width), F32))
        out_specs.append(whole(out_shape[1].shape))
    return call(
        functools.partial(band_kernel, with_ones), 1, [ANY, whole(counts.shape)] + [ANY] * 5, out_specs,
        out_shape, scratch, "band", cost(BAND_COST, 20 * 10**6), VMEM_BAND,
    )(offsets, ts, counts, below, low, high, above, band_weights)


def round_scratch(incoming, remote_weights, mixed):
    return [
        pltpu.VMEM(incoming.shape, BF16),
        pltpu.VMEM(remote_weights.shape, BF16),
        pltpu.VMEM(mixed.shape, F32),
        pltpu.VMEM(mixed.shape, F32),
    ]


def first_round(send, landing, incoming, remote_weights, mixed, columns):
    shards, rows, width = incoming.shape
    count_tiles = mixed.shape[0]
    tile, _ = shapes(count_tiles, rows, shards)
    recip = jax.ShapeDtypeStruct((count_tiles, width), F32)
    first = jax.ShapeDtypeStruct((8, width), F32)
    scratch = round_scratch(incoming, remote_weights, mixed) + [
        pltpu.VMEM(mixed.shape, BF16),
        pltpu.VMEM(columns.shape, F32),
        pltpu.VMEM(recip.shape, F32),
        pltpu.VMEM(first.shape, F32),
        pltpu.VMEM((EXTRA, width), F32),
        sems(PARTS + 2 * LOADS),
        sems(3 + PARTS),
    ]
    return call(
        first_kernel, 2, [ANY] * 4, [ANY] * 5, [tile, tile, first, recip, first], scratch, "first",
        cost(2 * 128 * 72 * 128 * 128, 20 * 10**6), VMEM_ROUND,
    )(send, landing, incoming, remote_weights, mixed, columns)


def last_round(landing, incoming, remote_weights, mixed, recip, first):
    rows, width = incoming.shape[1:]
    shape = (rows - EXTRA, mixed.shape[0] * width)
    scratch = round_scratch(incoming, remote_weights, mixed) + [
        pltpu.VMEM(shape, F32),
        pltpu.VMEM(recip.shape, F32),
        pltpu.VMEM(first.shape, F32),
        sems(PARTS + 2 * LOADS),
        sems(PARTS),
    ]
    return call(
        last_kernel, 1, [ANY] * 5, ANY, jax.ShapeDtypeStruct(shape, F32), scratch, "last",
        cost(2 * 128 * 72 * 128 * 128, 20 * 10**6), VMEM_ROUND,
    )(landing, incoming, remote_weights, mixed, recip, first)


def on_device(target_sums, counts, band_offsets, band_weights, send_tiles, landing_tiles, remote_weights):
    count_tiles, _, width, _ = band_weights.shape
    shards = remote_weights.shape[0]
    reach = count_tiles // 2
    counts = counts.reshape(count_tiles, width)
    send, landing, offsets = send_tiles.reshape(-1), landing_tiles.reshape(-1), band_offsets.reshape(-1)
    up = [(i, i + 1) for i in range(shards - 1)]
    down = [(i + 1, i) for i in range(shards - 1)]

    def exchange(low, high, block, *weights):
        below = lax.ppermute(high, "item", up)
        above = lax.ppermute(low, "item", down)
        outgoing = fill_messages(send, low, high, block, *weights)
        incoming = lax.all_to_all(outgoing, "item", split_axis=0, concat_axis=0, tiled=True)
        return below, above, incoming

    low, high, block = prep(target_sums, counts, shards)
    below, above, incoming = exchange(low, high, block, remote_weights)
    mixed, sums = band_product(True, offsets, target_sums, counts, below, low, high, above, band_weights)
    from_below = lax.ppermute(sums[reach + count_tiles :], "item", up)
    from_above = lax.ppermute(sums[:reach], "item", down)
    columns = sums[reach : reach + count_tiles] + jnp.concatenate([from_below, from_above], axis=0)
    low, high, block, recip, first = first_round(send, landing, incoming, remote_weights, mixed, columns)
    below, above, incoming = exchange(low, high, block)
    (mixed,) = band_product(False, offsets, target_sums, counts, below, low, high, above, band_weights)
    return last_round(landing, incoming, remote_weights, mixed, recip, first)


def solution(mesh):
    return jax.shard_map(
        on_device,
        mesh=mesh,
        in_specs=(
            P(None, "item"),
            P("item"),
            P("item", None),
            P("item", None, None, None),
            P("item", None),
            P("item", None),
            P("item", None, None),
        ),
        out_specs=P(None, "item"),
        check_vma=False,
    )
```

```python
import functools

import jax
import jax.numpy as jnp
from jax import lax
from jax.experimental import pallas as pl
from jax.experimental.pallas import tpu as pltpu
from jax.sharding import PartitionSpec as P

PRIOR = 20.0
EXTRA = 8
F32 = jnp.float32
BF16 = jnp.bfloat16
LOADS = 8
BAND_LOADS = 12
PARTS = 4
BAND_COST = 10**11
MESSAGE_COST = 10**6
VMEM = 60
VMEM_ROUND = 60
VMEM_BAND = 52
AHEAD = 3


def pieces(value, count):
    parts = []
    for _ in range(count):
        part = value.astype(BF16).astype(F32)
        parts.append(part)
        value = value - part
    return parts


def rows8(rows, base=None):
    width = 128
    index = lax.broadcasted_iota(jnp.int32, (EXTRA, width), 0)
    block = jnp.zeros((EXTRA, width), F32) if base is None else base
    for place, row in rows.items():
        block = jnp.where(index == place, row, block)
    return block


def to_row(column, shift=0):
    channels = column.shape[0]
    lane = lax.broadcasted_iota(jnp.int32, (channels, 128), 1)
    sub = lax.broadcasted_iota(jnp.int32, (channels, 128), 0)
    return jnp.sum(jnp.where(lane == sub + shift, column, 0.0), axis=0, keepdims=True)


def to_column(row, channels, shift=0):
    lane = lax.broadcasted_iota(jnp.int32, (channels, 128), 1)
    sub = lax.broadcasted_iota(jnp.int32, (channels, 128), 0)
    return jnp.sum(jnp.where(lane == sub + shift, row, 0.0), axis=1, keepdims=True)


def at_lane(scalar, place):
    lane = lax.broadcasted_iota(jnp.int32, (1, 128), 1)
    return jnp.where(lane == place, scalar, 0.0)


def pick_lane(row, place):
    lane = lax.broadcasted_iota(jnp.int32, (1, 128), 1)
    return jnp.sum(jnp.where(lane == place, row, 0.0), axis=1, keepdims=True)


def total(block):
    return jnp.sum(jnp.sum(block, axis=0, keepdims=True), axis=1, keepdims=True)


def stacked(top, bottom):
    return jnp.concatenate([top, bottom], axis=0).astype(BF16)


def product(tile, weights):
    return lax.dot_general(tile, weights, (((1,), (1,)), ((), ())), preferred_element_type=F32)


class Loads:
    def __init__(self, pairs, count, sems, first):
        self.parts, self.count = [], count
        for i in range(count):
            part = []
            for number, (source, target, axis) in enumerate(pairs):
                size = source.shape[axis] // count
                at = (slice(None),) * axis + (pl.ds(i * size, size),)
                sem = sems.at[first + i * len(pairs) + number]
                part.append(pltpu.make_async_copy(source.at[at], target.at[at], sem))
            self.parts.append(part)

    def start(self, i):
        if i < self.count:
            for copy in self.parts[i]:
                copy.start()

    def wait(self, i):
        for copy in self.parts[i]:
            copy.wait()


def two_products(tiles, weights):
    rows, width = tiles[0].shape
    both = product(jnp.concatenate(tiles, axis=0), jnp.concatenate(weights, axis=0))
    return both[:rows, :width], both[rows:, width:]


class Halves:
    def __init__(self, odd, tiles, half, inner_ref, outer_ref, sems, first, parts):
        self.odd, self.copies, size = odd, [], half // (parts // 2)
        for i in range(parts):
            source, at = tiles.at[pl.ds(i * size, size)], pl.ds(i * size % half, size)
            inner = pltpu.make_async_copy(source, inner_ref.at[at], sems.at[first + i])
            outer = pltpu.make_async_copy(source, outer_ref.at[at], sems.at[first + i])
            upper = i >= parts // 2
            self.copies.append((outer, inner) if upper else (inner, outer))

    def start(self, i):
        pl.when(self.odd == 1)(self.copies[i][0].start)
        pl.when(self.odd == 0)(self.copies[i][1].start)

    def wait(self, i):
        pl.when(self.odd == 1)(self.copies[i][0].wait)
        pl.when(self.odd == 0)(self.copies[i][1].wait)


def message_kernel(with_columns, odd_ref, send_ref, inner_ref, outer_ref, block_ref, *rest):
    if with_columns:
        remote_ref, out_ref, tiles, messages, block, sems, out_sems, remote, columns = rest
    else:
        out_ref, tiles, messages, block, sems, out_sems = rest
    count, rows, width = messages.shape
    half = inner_ref.shape[0]
    odd = odd_ref[0]
    loads = [
        pltpu.make_async_copy(inner_ref, tiles.at[pl.ds((1 - odd) * half, half)], sems.at[0]),
        pltpu.make_async_copy(outer_ref, tiles.at[pl.ds(odd * half, half)], sems.at[1]),
        pltpu.make_async_copy(block_ref, block, sems.at[2]),
    ]
    for load in loads:
        load.start()
    top = jnp.zeros((rows - EXTRA, width), F32)
    part = count // PARTS
    if with_columns:
        remote_loads = Loads([(remote_ref, remote, 0)], PARTS, sems, 3)
        for i in range(PARTS):
            remote_loads.start(i)
    for load in loads:
        load.wait()
    shared = block[...]
    stores = Loads([(messages, out_ref, 0)], PARTS, out_sems, 0)
    for number in range(PARTS):
        if with_columns:
            remote_loads.wait(number)

            def column(k, carry, number=number):
                q = number * part + k
                columns[pl.ds(q, 1), :] = jnp.sum(remote[q].astype(F32), axis=0, keepdims=True)
                return carry

            lax.fori_loop(0, part, column, 0, unroll=8)

        def step(k, carry, number=number):
            q = number * part + k
            extra = shared
            if with_columns:
                high, low = pieces(columns[pl.ds(q, 1), :], 2)
                extra = rows8({6: high, 7: low}, shared)
            messages[q] = tiles[send_ref[q]] + stacked(top, extra)
            return carry

        lax.fori_loop(0, part, step, 0, unroll=8)
        stores.start(number)
    for number in range(PARTS):
        stores.wait(number)


def prep_kernel(odd_ref, ts_ref, counts_ref, inner_ref, outer_ref, block_ref, ts, tiles, sems, out_sems):
    channels, width = ts.shape[0], counts_ref.shape[1]
    count_tiles = tiles.shape[0]
    half = count_tiles // 2
    here = count_tiles // LOADS
    loads = Loads([(ts_ref, ts, 1)], LOADS, sems, 0)
    for load in range(2 * AHEAD):
        loads.start(load)
    stores = Halves(odd_ref[0], tiles, half, inner_ref, outer_ref, out_sems, 0, PARTS)
    part = jnp.zeros((channels, width), F32)
    for load in range(LOADS):
        loads.wait(load)
        loads.start(load + 2 * AHEAD)

        def tile(k, part, load=load):
            t = load * here + k
            block = ts[:, pl.ds(pl.multiple_of(t * width, width), width)]
            count = counts_ref[pl.ds(t, 1), :].astype(F32)
            recip = 1.0 / (count + PRIOR)
            high, low = pieces(recip, 2)
            tiles[t] = stacked(block * recip, rows8({0: high, 1: low, 2: jnp.ones_like(recip)}))
            return part + block

        part = lax.fori_loop(0, here, tile, part, unroll=4)
        if (load + 1) % (LOADS // PARTS) == 0:
            stores.start(load // (LOADS // PARTS))
    row = to_row(jnp.sum(part, axis=1, keepdims=True))
    row = row + at_lane(total(counts_ref[...].astype(F32)), channels)
    one, two, three = pieces(row, 3)
    block_ref[...] = rows8({3: one, 4: two, 5: three})
    for i in range(PARTS):
        stores.wait(i)


def band_kernel(
    with_ones, odd_ref, offsets_ref, ts_ref, counts_ref, inner_ref, outer_ref, from_inner_ref, from_outer_ref,
    weights_ref, out_ref, *rest
):
    if with_ones:
        sums_ref, ts, weights, window, result, sems, out_sems = rest
    else:
        ts, weights, window, result, sems, out_sems = rest
    count_tiles, band = weights.shape[:2]
    reach, rows, width = inner_ref.shape
    channels = rows - EXTRA
    here = count_tiles // BAND_LOADS
    odd = odd_ref[0]
    parts = []
    for i, (ref, at) in enumerate(
        ((inner_ref, 2 - odd), (outer_ref, 1 + odd), (from_inner_ref, 3 - 3 * odd), (from_outer_ref, 3 * odd))
    ):
        copy = pltpu.make_async_copy(ref, window.at[pl.ds(at * reach, reach)], sems.at[2 * BAND_LOADS + i])
        copy.start()
        parts.append(copy)
    loads = Loads([(weights_ref, weights, 0), (ts_ref, ts, 1)], BAND_LOADS, sems, 0)
    for load in range(AHEAD):
        loads.start(load)
    if with_ones:
        sums_ref[...] = jnp.zeros_like(sums_ref)
    for copy in parts:
        copy.wait()
    if with_ones:
        sub = lax.broadcasted_iota(jnp.int32, (rows, width), 0)
        for begin in (0, reach + count_tiles):

            def fix(k, carry, begin=begin):
                value = window[begin + k].astype(F32)
                window[begin + k] = jnp.where(sub == channels + 2, 1.0, value).astype(BF16)
                return carry

            lax.fori_loop(0, reach, fix, 0, unroll=4)
    stores = Loads([(result, out_ref, 0)], BAND_LOADS, out_sems, 0)
    for load in range(BAND_LOADS):
        loads.start(load + AHEAD)
        loads.wait(load)

        def tile(k, carry, load=load):
            t = load * here + k
            places = [t + offsets_ref[t * band + b] + reach for b in range(band)]
            matrices = [weights[t, b] for b in range(band)]
            sources = jnp.concatenate([window[place] for place in places], axis=1)
            mixed = product(sources, jnp.concatenate(matrices, axis=1))
            known = [ts[:, pl.ds(pl.multiple_of(t * width, width), width)]]
            known.append(rows8({2: counts_ref[pl.ds(t, 1), :].astype(F32)}))
            result[t] = mixed + jnp.concatenate(known, axis=0)
            if with_ones:
                for place, matrix in zip(places, matrices):
                    sums_ref[pl.ds(place, 1), :] += jnp.sum(matrix.astype(F32), axis=0, keepdims=True)
            return carry

        lax.fori_loop(0, here, tile, 0, unroll=4)
        stores.start(load)
    for load in range(BAND_LOADS):
        stores.wait(load)


def add_remote(landing_ref, in_ref, weights_ref, band_ref, incoming, weights, band, acc, sems, each=None):
    shards, rows, width = incoming.shape
    group = shards // LOADS
    loads = Loads([(in_ref, incoming, 0), (weights_ref, weights, 0)], LOADS, sems, 0)
    band_loads = Loads([(band_ref, band, 0)], PARTS, sems, 2 * LOADS)
    for load in range(AHEAD):
        loads.start(load)

    def clear(t, carry):
        acc[t] = jnp.zeros((rows, width), F32)
        return carry

    lax.fori_loop(0, acc.shape[0], clear, 0, unroll=8)
    seen = jnp.zeros((EXTRA, width), F32)
    for load in range(LOADS):
        loads.start(load + AHEAD)
        if load + AHEAD >= LOADS:
            band_loads.start(load + AHEAD - LOADS)
        loads.wait(load)

        def pair(k, seen, load=load):
            p = load * group + 2 * k
            values = [incoming[p], incoming[p + 1]]
            tails = [value.astype(F32)[rows - EXTRA :] for value in values]
            mixed = two_products(values, [weights[p], weights[p + 1]])
            for i in range(2):
                acc[landing_ref[p + i]] += mixed[i]
                if each is not None:
                    each(p + i, tails[i])
            return seen + (tails[0] + tails[1])

        seen = lax.fori_loop(0, group // 2, pair, seen, unroll=8)
    for part in range(AHEAD, PARTS):
        band_loads.start(part)
    return seen, band_loads


def first_kernel(
    odd_ref, send_ref, landing_ref, in_ref, weights_ref, band_ref, columns_ref,
    inner_ref, outer_ref, block_ref, recip_ref, first_ref,
    incoming, weights, band, acc, tiles, columns, recips, firsts, block, sems, out_sems,
):
    shards, rows, width = incoming.shape
    channels = rows - EXTRA
    count_tiles = acc.shape[0]
    half = count_tiles // 2
    column_load = pltpu.make_async_copy(columns_ref, columns, out_sems.at[0])
    column_load.start()
    column_load.wait()

    def each(p, tail):
        columns[pl.ds(send_ref[p], 1), :] += tail[6:7] + tail[7:8]

    seen, band_loads = add_remote(
        landing_ref, in_ref, weights_ref, band_ref, incoming, weights, band, acc, sems, each
    )
    known = seen[3:4, :] + seen[4:5, :] + seen[5:6, :]
    count_total = pick_lane(known, channels)
    first = jnp.broadcast_to(PRIOR * to_column(known, channels) / count_total, (channels, width))
    firsts[...] = jnp.broadcast_to(known, firsts.shape)
    zero = jnp.zeros((channels, width), F32)
    line = jnp.zeros((1, width), F32)
    carry = (zero, zero, line, line)
    stores = []
    halves = Halves(odd_ref[0], tiles, half, inner_ref, outer_ref, out_sems, 3, PARTS)
    part = count_tiles // PARTS
    for number in range(PARTS):
        band_loads.wait(number)

        def finish(k, carry, number=number):
            t = number * part + k
            all_totals, all_states, all_weights, all_recips = carry
            mixed = acc[t] + band[t]
            spread = mixed[channels : channels + 1] + mixed[channels + 1 : channels + 2]
            totals = mixed[:channels] + first * spread
            weight = mixed[channels + 2 : channels + 3]
            recip = 1.0 / (weight + PRIOR)
            recips[pl.ds(t, 1), :] = recip
            high, low = pieces(recip, 2)
            state = (totals * recip).astype(BF16).astype(F32)
            tiles[t] = stacked(state, rows8({0: high, 1: low}))
            column = columns[pl.ds(t, 1), :]
            return (
                all_totals + totals,
                all_states + state * column,
                all_weights + weight,
                all_recips + (high + low) * column,
            )

        carry = lax.fori_loop(0, part, finish, carry, unroll=4)
        halves.start(number)
    all_totals, all_states, all_weights, all_recips = carry
    row = to_row(jnp.sum(all_totals, axis=1, keepdims=True))
    row = row + to_row(jnp.sum(all_states, axis=1, keepdims=True), channels)
    scalars = at_lane(total(all_weights), 0) + at_lane(total(all_recips), 1)
    one, two, three = pieces(row, 3)
    uno, due, tre = pieces(scalars, 3)
    block[...] = rows8({2: uno, 3: one, 4: two, 5: three, 6: due, 7: tre})
    for source, ref in ((recips, recip_ref), (firsts, first_ref), (block, block_ref)):
        stores.append(pltpu.make_async_copy(source, ref, out_sems.at[len(stores)]))
        stores[-1].start()
    for store in stores:
        store.wait()
    for number in range(PARTS):
        halves.wait(number)


def last_kernel(
    landing_ref, in_ref, weights_ref, band_ref, recip_ref, first_ref, out_ref,
    incoming, weights, band, acc, result, recips, firsts, sems, out_sems,
):
    shards, rows, width = incoming.shape
    channels = rows - EXTRA
    count_tiles = acc.shape[0]
    small = [
        pltpu.make_async_copy(recip_ref, recips, out_sems.at[0]),
        pltpu.make_async_copy(first_ref, firsts, out_sems.at[1]),
    ]
    for load in small:
        load.start()
    seen, band_loads = add_remote(
        landing_ref, in_ref, weights_ref, band_ref, incoming, weights, band, acc, sems
    )
    for load in small:
        load.wait()
    known = seen[3:4, :] + seen[4:5, :] + seen[5:6, :]
    scalars = seen[2:3, :] + seen[6:7, :] + seen[7:8, :]
    weight_total, spread_total = pick_lane(scalars, 0), pick_lane(scalars, 1)
    mean = PRIOR * to_column(known, channels) / weight_total
    mixed_total = to_column(known, channels, channels) + mean * spread_total
    last = PRIOR * (to_column(firsts[0:1, :], channels) + mixed_total) / weight_total
    mean, last = jnp.broadcast_to(mean, (channels, width)), jnp.broadcast_to(last, (channels, width))
    stores = []
    part = count_tiles // PARTS
    for number in range(PARTS):
        band_loads.wait(number)

        def finish(k, carry, number=number):
            t = number * part + k
            mixed = acc[t] + band[t]
            spread = mixed[channels : channels + 1] + mixed[channels + 1 : channels + 2]
            at = pl.ds(pl.multiple_of(t * width, width), width)
            result[:, at] = (mixed[:channels] + mean * spread + last) * recips[pl.ds(t, 1), :]
            return carry

        lax.fori_loop(0, part, finish, 0, unroll=4)
        at = pl.ds(number * part * width, part * width)
        stores.append(pltpu.make_async_copy(result.at[:, at], out_ref.at[:, at], out_sems.at[number]))
        stores[-1].start()
    for store in stores:
        store.wait()


def params(mib):
    return pltpu.CompilerParams(vmem_limit_bytes=mib * 2**20)


def cost(flops, size):
    return pl.CostEstimate(flops=flops, bytes_accessed=size, transcendentals=0)


def whole(shape):
    zeros = (0,) * len(shape)
    return pl.BlockSpec(shape, lambda *_: zeros)


ANY = pl.BlockSpec(memory_space=pl.ANY)


def shapes(count_tiles, rows, shards, width=128):
    tile = jax.ShapeDtypeStruct((count_tiles // 2, rows, width), BF16)
    message = jax.ShapeDtypeStruct((shards, rows, width), BF16)
    return tile, message


def call(kernel, prefetch, in_specs, out_specs, out_shape, scratch, name, estimate, limit=VMEM):
    return pl.pallas_call(
        kernel,
        grid_spec=pltpu.PrefetchScalarGridSpec(
            num_scalar_prefetch=prefetch,
            grid=(1,),
            in_specs=in_specs,
            out_specs=out_specs,
            scratch_shapes=scratch,
        ),
        out_shape=out_shape,
        compiler_params=params(limit),
        cost_estimate=estimate,
        name=name,
    )


def sems(count):
    return pltpu.SemaphoreType.DMA((count,))


def prep(odd, ts, counts, shards):
    channels, columns = ts.shape
    count_tiles, width = counts.shape
    rows = channels + EXTRA
    tile, _ = shapes(count_tiles, rows, shards)
    scratch = [pltpu.VMEM(ts.shape, F32), pltpu.VMEM((count_tiles, rows, width), BF16), sems(LOADS), sems(PARTS)]
    block = jax.ShapeDtypeStruct((EXTRA, width), F32)
    return call(
        prep_kernel, 1, [ANY, whole(counts.shape)], [ANY, ANY, whole(block.shape)], [tile, tile, block], scratch,
        "prep", cost(10**6, 5 * 10**6),
    )(odd, ts, counts)


def fill_messages(odd, send, inner, outer, block, remote_weights=None):
    half, rows, width = inner.shape
    shards = send.shape[0]
    _, message = shapes(2 * half, rows, shards)
    scratch = [
        pltpu.VMEM((2 * half, rows, width), BF16),
        pltpu.VMEM(message.shape, BF16),
        pltpu.VMEM(block.shape, F32),
        sems(3 + PARTS),
        sems(PARTS),
    ]
    operands = [odd, send, inner, outer, block]
    if remote_weights is not None:
        operands.append(remote_weights)
        scratch += [pltpu.VMEM(remote_weights.shape, BF16), pltpu.VMEM((shards, width), F32)]
    return call(
        functools.partial(message_kernel, remote_weights is not None), 2, [ANY] * (len(operands) - 2), ANY,
        message, scratch, "messages", cost(MESSAGE_COST, 5 * 10**6),
    )(*operands)


def band_product(with_ones, odd, offsets, ts, counts, inner, outer, from_inner, from_outer, band_weights):
    count_tiles, _, width, _ = band_weights.shape
    rows = inner.shape[1]
    shape = (count_tiles, rows, width)
    scratch = [
        pltpu.VMEM(ts.shape, F32),
        pltpu.VMEM(band_weights.shape, BF16),
        pltpu.VMEM((2 * count_tiles, rows, width), BF16),
        pltpu.VMEM(shape, F32),
        sems(2 * BAND_LOADS + 4),
        sems(BAND_LOADS),
    ]
    out_shape, out_specs = [jax.ShapeDtypeStruct(shape, F32)], [ANY]
    if with_ones:
        out_shape.append(jax.ShapeDtypeStruct((2 * count_tiles, width), F32))
        out_specs.append(whole(out_shape[1].shape))
    return call(
        functools.partial(band_kernel, with_ones), 2, [ANY, whole(counts.shape)] + [ANY] * 5, out_specs,
        out_shape, scratch, "band", cost(BAND_COST, 20 * 10**6), VMEM_BAND,
    )(odd, offsets, ts, counts, inner, outer, from_inner, from_outer, band_weights)


def round_scratch(incoming, remote_weights, mixed):
    return [
        pltpu.VMEM(incoming.shape, BF16),
        pltpu.VMEM(remote_weights.shape, BF16),
        pltpu.VMEM(mixed.shape, F32),
        pltpu.VMEM(mixed.shape, F32),
    ]


def first_round(odd, send, landing, incoming, remote_weights, mixed, columns):
    shards, rows, width = incoming.shape
    count_tiles = mixed.shape[0]
    tile, _ = shapes(count_tiles, rows, shards)
    recip = jax.ShapeDtypeStruct((count_tiles, width), F32)
    first = jax.ShapeDtypeStruct((8, width), F32)
    scratch = round_scratch(incoming, remote_weights, mixed) + [
        pltpu.VMEM(mixed.shape, BF16),
        pltpu.VMEM(columns.shape, F32),
        pltpu.VMEM(recip.shape, F32),
        pltpu.VMEM(first.shape, F32),
        pltpu.VMEM((EXTRA, width), F32),
        sems(PARTS + 2 * LOADS),
        sems(3 + PARTS),
    ]
    return call(
        first_kernel, 3, [ANY] * 4, [ANY] * 5, [tile, tile, first, recip, first], scratch, "first",
        cost(2 * 128 * 72 * 128 * 128, 20 * 10**6), VMEM_ROUND,
    )(odd, send, landing, incoming, remote_weights, mixed, columns)


def last_round(landing, incoming, remote_weights, mixed, recip, first):
    rows, width = incoming.shape[1:]
    shape = (rows - EXTRA, mixed.shape[0] * width)
    scratch = round_scratch(incoming, remote_weights, mixed) + [
        pltpu.VMEM(shape, F32),
        pltpu.VMEM(recip.shape, F32),
        pltpu.VMEM(first.shape, F32),
        sems(PARTS + 2 * LOADS),
        sems(PARTS),
    ]
    return call(
        last_kernel, 1, [ANY] * 5, ANY, jax.ShapeDtypeStruct(shape, F32), scratch, "last",
        cost(2 * 128 * 72 * 128 * 128, 20 * 10**6), VMEM_ROUND,
    )(landing, incoming, remote_weights, mixed, recip, first)


def on_device(target_sums, counts, band_offsets, band_weights, send_tiles, landing_tiles, remote_weights):
    count_tiles, _, width, _ = band_weights.shape
    shards = remote_weights.shape[0]
    reach = count_tiles // 2
    counts = counts.reshape(count_tiles, width)
    send, landing, offsets = send_tiles.reshape(-1), landing_tiles.reshape(-1), band_offsets.reshape(-1)
    parity = lax.axis_index("item") % 2
    odd = parity.reshape(1)
    inner_pairs = [(i, i ^ 1) for i in range(shards)]
    outer_pairs = [(i, i + 1 if i % 2 else i - 1) for i in range(1, shards - 1)]

    def swap(inner, outer):
        return lax.ppermute(inner, "item", inner_pairs), lax.ppermute(outer, "item", outer_pairs)

    def exchange(inner, outer, block, *weights):
        halo = swap(inner, outer)
        outgoing = fill_messages(odd, send, inner, outer, block, *weights)
        incoming = lax.all_to_all(outgoing, "item", split_axis=0, concat_axis=0, tiled=True)
        return halo, incoming

    inner, outer, block = prep(odd, target_sums, counts, shards)
    halo, incoming = exchange(inner, outer, block, remote_weights)
    mixed, sums = band_product(True, odd, offsets, target_sums, counts, inner, outer, *halo, band_weights)
    below, above = sums[:reach], sums[reach + count_tiles :]
    from_inner, from_outer = swap(
        jnp.where(parity == 1, below, above), jnp.where(parity == 1, above, below)
    )
    lower, upper = (
        jnp.where(parity == 1, from_inner, from_outer), jnp.where(parity == 1, from_outer, from_inner)
    )
    columns = sums[reach : reach + count_tiles] + jnp.concatenate([lower, upper], axis=0)
    inner, outer, block, recip, first = first_round(
        odd, send, landing, incoming, remote_weights, mixed, columns
    )
    halo, incoming = exchange(inner, outer, block)
    (mixed,) = band_product(False, odd, offsets, target_sums, counts, inner, outer, *halo, band_weights)
    return last_round(landing, incoming, remote_weights, mixed, recip, first)


def solution(mesh):
    return jax.shard_map(
        on_device,
        mesh=mesh,
        in_specs=(
            P(None, "item"),
            P("item"),
            P("item", None),
            P("item", None, None, None),
            P("item", None),
            P("item", None),
            P("item", None, None),
        ),
        out_specs=P(None, "item"),
        check_vma=False,
    )
```

```python
import functools

import jax
import jax.numpy as jnp
from jax import lax
from jax.experimental import pallas as pl
from jax.experimental.pallas import tpu as pltpu
from jax.sharding import PartitionSpec as P

PRIOR = 20.0
EXTRA = 8
F32 = jnp.float32
BF16 = jnp.bfloat16
LOADS = 8
BAND_LOADS = 12
PARTS = 4
MESSAGE_PARTS = 8
BAND_COST = 10**11
MESSAGE_COST = 10**6
VMEM = 60
VMEM_ROUND = 60
VMEM_BAND = 52
AHEAD = 3


def pieces(value, count):
    parts = []
    for _ in range(count):
        part = value.astype(BF16).astype(F32)
        parts.append(part)
        value = value - part
    return parts


def rows8(rows, base=None):
    width = 128
    index = lax.broadcasted_iota(jnp.int32, (EXTRA, width), 0)
    block = jnp.zeros((EXTRA, width), F32) if base is None else base
    for place, row in rows.items():
        block = jnp.where(index == place, row, block)
    return block


def to_row(column, shift=0):
    channels = column.shape[0]
    lane = lax.broadcasted_iota(jnp.int32, (channels, 128), 1)
    sub = lax.broadcasted_iota(jnp.int32, (channels, 128), 0)
    return jnp.sum(jnp.where(lane == sub + shift, column, 0.0), axis=0, keepdims=True)


def to_column(row, channels, shift=0):
    lane = lax.broadcasted_iota(jnp.int32, (channels, 128), 1)
    sub = lax.broadcasted_iota(jnp.int32, (channels, 128), 0)
    return jnp.sum(jnp.where(lane == sub + shift, row, 0.0), axis=1, keepdims=True)


def at_lane(scalar, place):
    lane = lax.broadcasted_iota(jnp.int32, (1, 128), 1)
    return jnp.where(lane == place, scalar, 0.0)


def pick_lane(row, place):
    lane = lax.broadcasted_iota(jnp.int32, (1, 128), 1)
    return jnp.sum(jnp.where(lane == place, row, 0.0), axis=1, keepdims=True)


def total(block):
    return jnp.sum(jnp.sum(block, axis=0, keepdims=True), axis=1, keepdims=True)


def stacked(top, bottom):
    return jnp.concatenate([top, bottom], axis=0).astype(BF16)


def product(tile, weights):
    return lax.dot_general(tile, weights, (((1,), (1,)), ((), ())), preferred_element_type=F32)


class Loads:
    def __init__(self, pairs, count, sems, first):
        self.parts, self.count = [], count
        for i in range(count):
            part = []
            for number, (source, target, axis) in enumerate(pairs):
                size = source.shape[axis] // count
                at = (slice(None),) * axis + (pl.ds(i * size, size),)
                sem = sems.at[first + i * len(pairs) + number]
                part.append(pltpu.make_async_copy(source.at[at], target.at[at], sem))
            self.parts.append(part)

    def start(self, i):
        if i < self.count:
            for copy in self.parts[i]:
                copy.start()

    def wait(self, i):
        for copy in self.parts[i]:
            copy.wait()


def two_products(tiles, weights):
    rows, width = tiles[0].shape
    both = product(jnp.concatenate(tiles, axis=0), jnp.concatenate(weights, axis=0))
    return both[:rows, :width], both[rows:, width:]


class Halves:
    def __init__(self, odd, tiles, half, inner_ref, outer_ref, sems, first, parts):
        self.odd, self.copies, size = odd, [], half // (parts // 2)
        for i in range(parts):
            source, at = tiles.at[pl.ds(i * size, size)], pl.ds(i * size % half, size)
            inner = pltpu.make_async_copy(source, inner_ref.at[at], sems.at[first + i])
            outer = pltpu.make_async_copy(source, outer_ref.at[at], sems.at[first + i])
            upper = i >= parts // 2
            self.copies.append((outer, inner) if upper else (inner, outer))

    def start(self, i):
        pl.when(self.odd == 1)(self.copies[i][0].start)
        pl.when(self.odd == 0)(self.copies[i][1].start)

    def wait(self, i):
        pl.when(self.odd == 1)(self.copies[i][0].wait)
        pl.when(self.odd == 0)(self.copies[i][1].wait)


def message_kernel(with_columns, odd_ref, send_ref, inner_ref, outer_ref, block_ref, *rest):
    if with_columns:
        remote_ref, out_ref, tiles, messages, block, sems, out_sems, remote, columns = rest
    else:
        out_ref, tiles, messages, block, sems, out_sems = rest
    count, rows, width = messages.shape
    half = inner_ref.shape[0]
    odd = odd_ref[0]
    loads = [
        pltpu.make_async_copy(inner_ref, tiles.at[pl.ds((1 - odd) * half, half)], sems.at[0]),
        pltpu.make_async_copy(outer_ref, tiles.at[pl.ds(odd * half, half)], sems.at[1]),
        pltpu.make_async_copy(block_ref, block, sems.at[2]),
    ]
    for load in loads:
        load.start()
    top = jnp.zeros((rows - EXTRA, width), F32)
    part = count // MESSAGE_PARTS
    if with_columns:
        remote_loads = Loads([(remote_ref, remote, 0)], MESSAGE_PARTS, sems, 3)
        for i in range(MESSAGE_PARTS):
            remote_loads.start(i)
    for load in loads:
        load.wait()
    shared = block[...]
    stores = Loads([(messages, out_ref, 0)], MESSAGE_PARTS, out_sems, 0)
    for number in range(MESSAGE_PARTS):
        if with_columns:
            remote_loads.wait(number)

            def column(k, carry, number=number):
                q = number * part + k
                columns[pl.ds(q, 1), :] = jnp.sum(remote[q].astype(F32), axis=0, keepdims=True)
                return carry

            lax.fori_loop(0, part, column, 0, unroll=8)

        def step(k, carry, number=number):
            q = number * part + k
            extra = shared
            if with_columns:
                high, low = pieces(columns[pl.ds(q, 1), :], 2)
                extra = rows8({6: high, 7: low}, shared)
            messages[q] = tiles[send_ref[q]] + stacked(top, extra)
            return carry

        lax.fori_loop(0, part, step, 0, unroll=8)
        stores.start(number)
    for number in range(MESSAGE_PARTS):
        stores.wait(number)


def prep_kernel(
    odd_ref, ts_ref, counts_ref, inner_ref, outer_ref, block_ref, ts, counts, tiles, block, sems, out_sems
):
    channels, width = ts.shape[0], counts.shape[1]
    count_tiles = tiles.shape[0]
    half = count_tiles // 2
    here = count_tiles // LOADS
    loads = Loads([(ts_ref, ts, 1)], LOADS, sems, 0)
    count_load = pltpu.make_async_copy(counts_ref, counts, sems.at[LOADS])
    count_load.start()
    for load in range(LOADS):
        loads.start(load)
    stores = Halves(odd_ref[0], tiles, half, inner_ref, outer_ref, out_sems, 0, PARTS)
    count_load.wait()
    part = jnp.zeros((channels, width), F32)
    for load in range(LOADS):
        loads.wait(load)

        def tile(k, part, load=load):
            t = load * here + k
            values = ts[:, pl.ds(pl.multiple_of(t * width, width), width)]
            count = counts[pl.ds(t, 1), :].astype(F32)
            recip = 1.0 / (count + PRIOR)
            high, low = pieces(recip, 2)
            tiles[t] = stacked(values * recip, rows8({0: high, 1: low, 2: jnp.ones_like(recip)}))
            return part + values

        part = lax.fori_loop(0, here, tile, part, unroll=4)
        if (load + 1) % (LOADS // PARTS) == 0:
            stores.start(load // (LOADS // PARTS))
    row = to_row(jnp.sum(part, axis=1, keepdims=True))
    row = row + at_lane(total(counts[...].astype(F32)), channels)
    one, two, three = pieces(row, 3)
    block[...] = rows8({3: one, 4: two, 5: three})
    block_store = pltpu.make_async_copy(block, block_ref, sems.at[LOADS])
    block_store.start()
    block_store.wait()
    for i in range(PARTS):
        stores.wait(i)


def band_kernel(
    with_ones, odd_ref, offsets_ref, ts_ref, counts_ref, inner_ref, outer_ref, from_inner_ref, from_outer_ref,
    weights_ref, out_ref, *rest
):
    if with_ones:
        sums_ref, ts, weights, window, result, sems, out_sems = rest
    else:
        ts, weights, window, result, sems, out_sems = rest
    count_tiles, band = weights.shape[:2]
    reach, rows, width = inner_ref.shape
    channels = rows - EXTRA
    here = count_tiles // BAND_LOADS
    odd = odd_ref[0]
    parts = []
    for i, (ref, at) in enumerate(
        ((inner_ref, 2 - odd), (outer_ref, 1 + odd), (from_inner_ref, 3 - 3 * odd), (from_outer_ref, 3 * odd))
    ):
        copy = pltpu.make_async_copy(ref, window.at[pl.ds(at * reach, reach)], sems.at[2 * BAND_LOADS + i])
        copy.start()
        parts.append(copy)
    loads = Loads([(weights_ref, weights, 0), (ts_ref, ts, 1)], BAND_LOADS, sems, 0)
    for load in range(AHEAD):
        loads.start(load)
    if with_ones:
        sums_ref[...] = jnp.zeros_like(sums_ref)
    for copy in parts:
        copy.wait()
    if with_ones:
        sub = lax.broadcasted_iota(jnp.int32, (rows, width), 0)
        for begin in (0, reach + count_tiles):

            def fix(k, carry, begin=begin):
                value = window[begin + k].astype(F32)
                window[begin + k] = jnp.where(sub == channels + 2, 1.0, value).astype(BF16)
                return carry

            lax.fori_loop(0, reach, fix, 0, unroll=4)
    stores = Loads([(result, out_ref, 0)], BAND_LOADS, out_sems, 0)
    for load in range(BAND_LOADS):
        loads.start(load + AHEAD)
        loads.wait(load)

        def tile(k, carry, load=load):
            t = load * here + k
            places = [t + offsets_ref[t * band + b] + reach for b in range(band)]
            matrices = [weights[t, b] for b in range(band)]
            sources = jnp.concatenate([window[place] for place in places], axis=1)
            mixed = product(sources, jnp.concatenate(matrices, axis=1))
            known = [ts[:, pl.ds(pl.multiple_of(t * width, width), width)]]
            known.append(rows8({2: counts_ref[pl.ds(t, 1), :].astype(F32)}))
            result[t] = mixed + jnp.concatenate(known, axis=0)
            if with_ones:
                for place, matrix in zip(places, matrices):
                    sums_ref[pl.ds(place, 1), :] += jnp.sum(matrix.astype(F32), axis=0, keepdims=True)
            return carry

        lax.fori_loop(0, here, tile, 0, unroll=4)
        stores.start(load)
    for load in range(BAND_LOADS):
        stores.wait(load)


def add_remote(landing_ref, in_ref, weights_ref, band_ref, incoming, weights, band, acc, sems, each=None, small=()):
    shards, rows, width = incoming.shape
    group = shards // LOADS
    loads = Loads([(in_ref, incoming, 0), (weights_ref, weights, 0)], LOADS, sems, 0)
    band_loads = Loads([(band_ref, band, 0)], PARTS, sems, 2 * LOADS)
    for load in range(AHEAD):
        loads.start(load)
    for load in small:
        load.start()

    def clear(t, carry):
        acc[t] = jnp.zeros((rows, width), F32)
        return carry

    lax.fori_loop(0, acc.shape[0], clear, 0, unroll=8)
    for load in small:
        load.wait()
    seen = jnp.zeros((EXTRA, width), F32)
    for load in range(LOADS):
        loads.start(load + AHEAD)
        if load + AHEAD >= LOADS:
            band_loads.start(load + AHEAD - LOADS)
        loads.wait(load)

        def pair(k, seen, load=load):
            p = load * group + 2 * k
            values = [incoming[p], incoming[p + 1]]
            tails = [value.astype(F32)[rows - EXTRA :] for value in values]
            mixed = two_products(values, [weights[p], weights[p + 1]])
            for i in range(2):
                acc[landing_ref[p + i]] += mixed[i]
                if each is not None:
                    each(p + i, tails[i])
            return seen + (tails[0] + tails[1])

        seen = lax.fori_loop(0, group // 2, pair, seen, unroll=8)
    for part in range(AHEAD, PARTS):
        band_loads.start(part)
    return seen, band_loads


def first_kernel(
    odd_ref, send_ref, landing_ref, in_ref, weights_ref, band_ref, columns_ref,
    inner_ref, outer_ref, block_ref, recip_ref, first_ref,
    incoming, weights, band, acc, tiles, columns, recips, firsts, block, sems, out_sems,
):
    shards, rows, width = incoming.shape
    channels = rows - EXTRA
    count_tiles = acc.shape[0]
    half = count_tiles // 2
    column_load = pltpu.make_async_copy(columns_ref, columns, out_sems.at[0])

    def each(p, tail):
        columns[pl.ds(send_ref[p], 1), :] += tail[6:7] + tail[7:8]

    seen, band_loads = add_remote(
        landing_ref, in_ref, weights_ref, band_ref, incoming, weights, band, acc, sems, each, [column_load]
    )
    known = seen[3:4, :] + seen[4:5, :] + seen[5:6, :]
    count_total = pick_lane(known, channels)
    first = jnp.broadcast_to(PRIOR * to_column(known, channels) / count_total, (channels, width))
    firsts[...] = jnp.broadcast_to(known, firsts.shape)
    zero = jnp.zeros((channels, width), F32)
    line = jnp.zeros((1, width), F32)
    carry = (zero, zero, line, line)
    stores = []
    halves = Halves(odd_ref[0], tiles, half, inner_ref, outer_ref, out_sems, 3, PARTS)
    part = count_tiles // PARTS
    for number in range(PARTS):
        band_loads.wait(number)

        def finish(k, carry, number=number):
            t = number * part + k
            all_totals, all_states, all_weights, all_recips = carry
            mixed = acc[t] + band[t]
            spread = mixed[channels : channels + 1] + mixed[channels + 1 : channels + 2]
            totals = mixed[:channels] + first * spread
            weight = mixed[channels + 2 : channels + 3]
            recip = 1.0 / (weight + PRIOR)
            recips[pl.ds(t, 1), :] = recip
            high, low = pieces(recip, 2)
            state = (totals * recip).astype(BF16).astype(F32)
            tiles[t] = stacked(state, rows8({0: high, 1: low}))
            column = columns[pl.ds(t, 1), :]
            return (
                all_totals + totals,
                all_states + state * column,
                all_weights + weight,
                all_recips + (high + low) * column,
            )

        carry = lax.fori_loop(0, part, finish, carry, unroll=4)
        halves.start(number)
    all_totals, all_states, all_weights, all_recips = carry
    row = to_row(jnp.sum(all_totals, axis=1, keepdims=True))
    row = row + to_row(jnp.sum(all_states, axis=1, keepdims=True), channels)
    scalars = at_lane(total(all_weights), 0) + at_lane(total(all_recips), 1)
    one, two, three = pieces(row, 3)
    uno, due, tre = pieces(scalars, 3)
    block[...] = rows8({2: uno, 3: one, 4: two, 5: three, 6: due, 7: tre})
    for source, ref in ((recips, recip_ref), (firsts, first_ref), (block, block_ref)):
        stores.append(pltpu.make_async_copy(source, ref, out_sems.at[len(stores)]))
        stores[-1].start()
    for store in stores:
        store.wait()
    for number in range(PARTS):
        halves.wait(number)


def last_kernel(
    landing_ref, in_ref, weights_ref, band_ref, recip_ref, first_ref, out_ref,
    incoming, weights, band, acc, result, recips, firsts, sems, out_sems,
):
    shards, rows, width = incoming.shape
    channels = rows - EXTRA
    count_tiles = acc.shape[0]
    small = [
        pltpu.make_async_copy(recip_ref, recips, out_sems.at[0]),
        pltpu.make_async_copy(first_ref, firsts, out_sems.at[1]),
    ]
    seen, band_loads = add_remote(
        landing_ref, in_ref, weights_ref, band_ref, incoming, weights, band, acc, sems, None, small
    )
    known = seen[3:4, :] + seen[4:5, :] + seen[5:6, :]
    scalars = seen[2:3, :] + seen[6:7, :] + seen[7:8, :]
    weight_total, spread_total = pick_lane(scalars, 0), pick_lane(scalars, 1)
    mean = PRIOR * to_column(known, channels) / weight_total
    mixed_total = to_column(known, channels, channels) + mean * spread_total
    last = PRIOR * (to_column(firsts[0:1, :], channels) + mixed_total) / weight_total
    mean, last = jnp.broadcast_to(mean, (channels, width)), jnp.broadcast_to(last, (channels, width))
    stores = []
    part = count_tiles // PARTS
    for number in range(PARTS):
        band_loads.wait(number)

        def finish(k, carry, number=number):
            t = number * part + k
            mixed = acc[t] + band[t]
            spread = mixed[channels : channels + 1] + mixed[channels + 1 : channels + 2]
            at = pl.ds(pl.multiple_of(t * width, width), width)
            result[:, at] = (mixed[:channels] + mean * spread + last) * recips[pl.ds(t, 1), :]
            return carry

        lax.fori_loop(0, part, finish, 0, unroll=4)
        at = pl.ds(number * part * width, part * width)
        stores.append(pltpu.make_async_copy(result.at[:, at], out_ref.at[:, at], out_sems.at[number]))
        stores[-1].start()
    for store in stores:
        store.wait()


def params(mib):
    return pltpu.CompilerParams(vmem_limit_bytes=mib * 2**20)


def cost(flops, size):
    return pl.CostEstimate(flops=flops, bytes_accessed=size, transcendentals=0)


def whole(shape):
    zeros = (0,) * len(shape)
    return pl.BlockSpec(shape, lambda *_: zeros)


ANY = pl.BlockSpec(memory_space=pl.ANY)


def shapes(count_tiles, rows, shards, width=128):
    tile = jax.ShapeDtypeStruct((count_tiles // 2, rows, width), BF16)
    message = jax.ShapeDtypeStruct((shards, rows, width), BF16)
    return tile, message


def call(kernel, prefetch, in_specs, out_specs, out_shape, scratch, name, estimate, limit=VMEM):
    return pl.pallas_call(
        kernel,
        grid_spec=pltpu.PrefetchScalarGridSpec(
            num_scalar_prefetch=prefetch,
            grid=(1,),
            in_specs=in_specs,
            out_specs=out_specs,
            scratch_shapes=scratch,
        ),
        out_shape=out_shape,
        compiler_params=params(limit),
        cost_estimate=estimate,
        name=name,
    )


def sems(count):
    return pltpu.SemaphoreType.DMA((count,))


def prep(odd, ts, counts, shards):
    channels, columns = ts.shape
    count_tiles, width = counts.shape
    rows = channels + EXTRA
    tile, _ = shapes(count_tiles, rows, shards)
    block = jax.ShapeDtypeStruct((EXTRA, width), F32)
    scratch = [
        pltpu.VMEM(ts.shape, F32),
        pltpu.VMEM(counts.shape, jnp.int32),
        pltpu.VMEM((count_tiles, rows, width), BF16),
        pltpu.VMEM(block.shape, F32),
        sems(LOADS + 1),
        sems(PARTS),
    ]
    return call(
        prep_kernel, 1, [ANY] * 2, [ANY] * 3, [tile, tile, block], scratch,
        "prep", cost(10**6, 5 * 10**6),
    )(odd, ts, counts)


def fill_messages(odd, send, inner, outer, block, remote_weights=None):
    half, rows, width = inner.shape
    shards = send.shape[0]
    _, message = shapes(2 * half, rows, shards)
    scratch = [
        pltpu.VMEM((2 * half, rows, width), BF16),
        pltpu.VMEM(message.shape, BF16),
        pltpu.VMEM(block.shape, F32),
        sems(3 + MESSAGE_PARTS),
        sems(MESSAGE_PARTS),
    ]
    operands = [odd, send, inner, outer, block]
    if remote_weights is not None:
        operands.append(remote_weights)
        scratch += [pltpu.VMEM(remote_weights.shape, BF16), pltpu.VMEM((shards, width), F32)]
    return call(
        functools.partial(message_kernel, remote_weights is not None), 2, [ANY] * (len(operands) - 2), ANY,
        message, scratch, "messages", cost(MESSAGE_COST, 5 * 10**6),
    )(*operands)


def band_product(with_ones, odd, offsets, ts, counts, inner, outer, from_inner, from_outer, band_weights):
    count_tiles, _, width, _ = band_weights.shape
    rows = inner.shape[1]
    shape = (count_tiles, rows, width)
    scratch = [
        pltpu.VMEM(ts.shape, F32),
        pltpu.VMEM(band_weights.shape, BF16),
        pltpu.VMEM((2 * count_tiles, rows, width), BF16),
        pltpu.VMEM(shape, F32),
        sems(2 * BAND_LOADS + 4),
        sems(BAND_LOADS),
    ]
    out_shape, out_specs = [jax.ShapeDtypeStruct(shape, F32)], [ANY]
    if with_ones:
        out_shape.append(jax.ShapeDtypeStruct((2 * count_tiles, width), F32))
        out_specs.append(whole(out_shape[1].shape))
    return call(
        functools.partial(band_kernel, with_ones), 2, [ANY, whole(counts.shape)] + [ANY] * 5, out_specs,
        out_shape, scratch, "band", cost(BAND_COST, 20 * 10**6), VMEM_BAND,
    )(odd, offsets, ts, counts, inner, outer, from_inner, from_outer, band_weights)


def round_scratch(incoming, remote_weights, mixed):
    return [
        pltpu.VMEM(incoming.shape, BF16),
        pltpu.VMEM(remote_weights.shape, BF16),
        pltpu.VMEM(mixed.shape, F32),
        pltpu.VMEM(mixed.shape, F32),
    ]


def first_round(odd, send, landing, incoming, remote_weights, mixed, columns):
    shards, rows, width = incoming.shape
    count_tiles = mixed.shape[0]
    tile, _ = shapes(count_tiles, rows, shards)
    recip = jax.ShapeDtypeStruct((count_tiles, width), F32)
    first = jax.ShapeDtypeStruct((8, width), F32)
    scratch = round_scratch(incoming, remote_weights, mixed) + [
        pltpu.VMEM(mixed.shape, BF16),
        pltpu.VMEM(columns.shape, F32),
        pltpu.VMEM(recip.shape, F32),
        pltpu.VMEM(first.shape, F32),
        pltpu.VMEM((EXTRA, width), F32),
        sems(PARTS + 2 * LOADS),
        sems(3 + PARTS),
    ]
    return call(
        first_kernel, 3, [ANY] * 4, [ANY] * 5, [tile, tile, first, recip, first], scratch, "first",
        cost(2 * 128 * 72 * 128 * 128, 20 * 10**6), VMEM_ROUND,
    )(odd, send, landing, incoming, remote_weights, mixed, columns)


def last_round(landing, incoming, remote_weights, mixed, recip, first):
    rows, width = incoming.shape[1:]
    shape = (rows - EXTRA, mixed.shape[0] * width)
    scratch = round_scratch(incoming, remote_weights, mixed) + [
        pltpu.VMEM(shape, F32),
        pltpu.VMEM(recip.shape, F32),
        pltpu.VMEM(first.shape, F32),
        sems(PARTS + 2 * LOADS),
        sems(PARTS),
    ]
    return call(
        last_kernel, 1, [ANY] * 5, ANY, jax.ShapeDtypeStruct(shape, F32), scratch, "last",
        cost(2 * 128 * 72 * 128 * 128, 20 * 10**6), VMEM_ROUND,
    )(landing, incoming, remote_weights, mixed, recip, first)


def on_device(target_sums, counts, band_offsets, band_weights, send_tiles, landing_tiles, remote_weights):
    count_tiles, _, width, _ = band_weights.shape
    shards = remote_weights.shape[0]
    reach = count_tiles // 2
    counts = counts.reshape(count_tiles, width)
    send, landing, offsets = send_tiles.reshape(-1), landing_tiles.reshape(-1), band_offsets.reshape(-1)
    parity = lax.axis_index("item") % 2
    odd = parity.reshape(1)
    inner_pairs = [(i, i ^ 1) for i in range(shards)]
    outer_pairs = [(i, i + 1 if i % 2 else i - 1) for i in range(1, shards - 1)]

    def swap(inner, outer):
        return lax.ppermute(inner, "item", inner_pairs), lax.ppermute(outer, "item", outer_pairs)

    def exchange(inner, outer, block, *weights):
        halo = swap(inner, outer)
        outgoing = fill_messages(odd, send, inner, outer, block, *weights)
        incoming = lax.all_to_all(outgoing, "item", split_axis=0, concat_axis=0, tiled=True)
        return halo, incoming

    inner, outer, block = prep(odd, target_sums, counts, shards)
    halo, incoming = exchange(inner, outer, block, remote_weights)
    mixed, sums = band_product(True, odd, offsets, target_sums, counts, inner, outer, *halo, band_weights)
    below, above = sums[:reach], sums[reach + count_tiles :]
    from_inner, from_outer = swap(
        jnp.where(parity == 1, below, above), jnp.where(parity == 1, above, below)
    )
    lower, upper = (
        jnp.where(parity == 1, from_inner, from_outer), jnp.where(parity == 1, from_outer, from_inner)
    )
    columns = sums[reach : reach + count_tiles] + jnp.concatenate([lower, upper], axis=0)
    inner, outer, block, recip, first = first_round(
        odd, send, landing, incoming, remote_weights, mixed, columns
    )
    halo, incoming = exchange(inner, outer, block)
    (mixed,) = band_product(False, odd, offsets, target_sums, counts, inner, outer, *halo, band_weights)
    return last_round(landing, incoming, remote_weights, mixed, recip, first)


def solution(mesh):
    return jax.shard_map(
        on_device,
        mesh=mesh,
        in_specs=(
            P(None, "item"),
            P("item"),
            P("item", None),
            P("item", None, None, None),
            P("item", None),
            P("item", None),
            P("item", None, None),
        ),
        out_specs=P(None, "item"),
        check_vma=False,
    )
```

```python
import functools

import jax
import jax.numpy as jnp
from jax import lax
from jax.experimental import pallas as pl
from jax.experimental.pallas import tpu as pltpu
from jax.sharding import PartitionSpec as P

PRIOR = 20.0
EXTRA = 8
F32 = jnp.float32
BF16 = jnp.bfloat16
LOADS = 8
BAND_LOADS = 12
PARTS = 4
MESSAGE_PARTS = 8
BAND_COST = 10**11
VMEM = 60
VMEM_ROUND = 60
VMEM_BAND = 52
AHEAD = 3


def pieces(value, count):
    parts = []
    for _ in range(count):
        part = value.astype(BF16).astype(F32)
        parts.append(part)
        value = value - part
    return parts


def rows8(rows, base=None):
    width = 128
    index = lax.broadcasted_iota(jnp.int32, (EXTRA, width), 0)
    block = jnp.zeros((EXTRA, width), F32) if base is None else base
    for place, row in rows.items():
        block = jnp.where(index == place, row, block)
    return block


def to_row(column, shift=0):
    channels = column.shape[0]
    lane = lax.broadcasted_iota(jnp.int32, (channels, 128), 1)
    sub = lax.broadcasted_iota(jnp.int32, (channels, 128), 0)
    return jnp.sum(jnp.where(lane == sub + shift, column, 0.0), axis=0, keepdims=True)


def to_column(row, channels, shift=0):
    lane = lax.broadcasted_iota(jnp.int32, (channels, 128), 1)
    sub = lax.broadcasted_iota(jnp.int32, (channels, 128), 0)
    return jnp.sum(jnp.where(lane == sub + shift, row, 0.0), axis=1, keepdims=True)


def at_lane(scalar, place):
    lane = lax.broadcasted_iota(jnp.int32, (1, 128), 1)
    return jnp.where(lane == place, scalar, 0.0)


def pick_lane(row, place):
    lane = lax.broadcasted_iota(jnp.int32, (1, 128), 1)
    return jnp.sum(jnp.where(lane == place, row, 0.0), axis=1, keepdims=True)


def total(block):
    return jnp.sum(jnp.sum(block, axis=0, keepdims=True), axis=1, keepdims=True)


def stacked(top, bottom):
    return jnp.concatenate([top, bottom], axis=0).astype(BF16)


def product(tile, weights):
    return lax.dot_general(tile, weights, (((1,), (1,)), ((), ())), preferred_element_type=F32)


class Loads:
    def __init__(self, pairs, count, sems, first):
        self.parts, self.count = [], count
        for i in range(count):
            part = []
            for number, (source, target, axis) in enumerate(pairs):
                size = source.shape[axis] // count
                at = (slice(None),) * axis + (pl.ds(i * size, size),)
                sem = sems.at[first + i * len(pairs) + number]
                part.append(pltpu.make_async_copy(source.at[at], target.at[at], sem))
            self.parts.append(part)

    def start(self, i):
        if i < self.count:
            for copy in self.parts[i]:
                copy.start()

    def wait(self, i):
        for copy in self.parts[i]:
            copy.wait()


def two_products(tiles, weights):
    rows, width = tiles[0].shape
    both = product(jnp.concatenate(tiles, axis=0), jnp.concatenate(weights, axis=0))
    return both[:rows, :width], both[rows:, width:]


class Halves:
    def __init__(self, odd, tiles, half, inner_ref, outer_ref, sems, first, parts):
        self.odd, self.copies, size = odd, [], half // (parts // 2)
        for i in range(parts):
            source, at = tiles.at[pl.ds(i * size, size)], pl.ds(i * size % half, size)
            inner = pltpu.make_async_copy(source, inner_ref.at[at], sems.at[first + i])
            outer = pltpu.make_async_copy(source, outer_ref.at[at], sems.at[first + i])
            upper = i >= parts // 2
            self.copies.append((outer, inner) if upper else (inner, outer))

    def start(self, i):
        pl.when(self.odd == 1)(self.copies[i][0].start)
        pl.when(self.odd == 0)(self.copies[i][1].start)

    def wait(self, i):
        pl.when(self.odd == 1)(self.copies[i][0].wait)
        pl.when(self.odd == 0)(self.copies[i][1].wait)


def store_messages(send_ref, tiles, messages, out_ref, sems, first, shared, remote=None, remote_loads=None):
    count, rows, width = messages.shape
    top = jnp.zeros((rows - EXTRA, width), F32)
    part = count // MESSAGE_PARTS
    stores = Loads([(messages, out_ref, 0)], MESSAGE_PARTS, sems, first)
    for number in range(MESSAGE_PARTS):
        if remote is not None:
            remote_loads.wait(number)

        def step(k, carry, number=number):
            q = number * part + k
            extra = shared
            if remote is not None:
                high, low = pieces(jnp.sum(remote[q].astype(F32), axis=0, keepdims=True), 2)
                extra = rows8({6: high, 7: low}, shared)
            messages[q] = tiles[send_ref[q]] + stacked(top, extra)
            return carry

        lax.fori_loop(0, part, step, 0, unroll=8)
        stores.start(number)
    return stores


def prep_kernel(
    odd_ref, send_ref, ts_ref, counts_ref, remote_ref, inner_ref, outer_ref, out_ref,
    ts, counts, remote, tiles, messages, sems, out_sems,
):
    channels, width = ts.shape[0], counts.shape[1]
    count_tiles = tiles.shape[0]
    half = count_tiles // 2
    here = count_tiles // LOADS
    loads = Loads([(ts_ref, ts, 1)], LOADS, sems, 0)
    count_load = pltpu.make_async_copy(counts_ref, counts, sems.at[LOADS])
    count_load.start()
    remote_loads = Loads([(remote_ref, remote, 0)], MESSAGE_PARTS, sems, LOADS + 1)
    for load in range(LOADS):
        loads.start(load)
    stores = Halves(odd_ref[0], tiles, half, inner_ref, outer_ref, out_sems, 0, PARTS)
    count_load.wait()
    part = jnp.zeros((channels, width), F32)
    for load in range(LOADS):
        loads.wait(load)
        if load >= LOADS // 2:
            for i in range(2):
                remote_loads.start(2 * (load - LOADS // 2) + i)

        def tile(k, part, load=load):
            t = load * here + k
            values = ts[:, pl.ds(pl.multiple_of(t * width, width), width)]
            count = counts[pl.ds(t, 1), :].astype(F32)
            recip = 1.0 / (count + PRIOR)
            high, low = pieces(recip, 2)
            tiles[t] = stacked(values * recip, rows8({0: high, 1: low, 2: jnp.ones_like(recip)}))
            return part + values

        part = lax.fori_loop(0, here, tile, part, unroll=4)
        if (load + 1) % (LOADS // PARTS) == 0:
            stores.start(load // (LOADS // PARTS))
    row = to_row(jnp.sum(part, axis=1, keepdims=True))
    row = row + at_lane(total(counts[...].astype(F32)), channels)
    one, two, three = pieces(row, 3)
    block = rows8({3: one, 4: two, 5: three})
    messages_out = store_messages(
        send_ref, tiles, messages, out_ref, out_sems, PARTS, block, remote, remote_loads
    )
    for i in range(PARTS):
        stores.wait(i)
    for i in range(MESSAGE_PARTS):
        messages_out.wait(i)


def band_kernel(
    with_ones, odd_ref, offsets_ref, ts_ref, counts_ref, inner_ref, outer_ref, from_inner_ref, from_outer_ref,
    weights_ref, out_ref, *rest
):
    if with_ones:
        sums_ref, ts, weights, window, result, sems, out_sems = rest
    else:
        ts, weights, window, result, sems, out_sems = rest
    count_tiles, band = weights.shape[:2]
    reach, rows, width = inner_ref.shape
    channels = rows - EXTRA
    here = count_tiles // BAND_LOADS
    odd = odd_ref[0]
    parts = []
    for i, (ref, at) in enumerate(
        ((inner_ref, 2 - odd), (outer_ref, 1 + odd), (from_inner_ref, 3 - 3 * odd), (from_outer_ref, 3 * odd))
    ):
        copy = pltpu.make_async_copy(ref, window.at[pl.ds(at * reach, reach)], sems.at[2 * BAND_LOADS + i])
        copy.start()
        parts.append(copy)
    loads = Loads([(weights_ref, weights, 0), (ts_ref, ts, 1)], BAND_LOADS, sems, 0)
    for load in range(AHEAD):
        loads.start(load)
    if with_ones:
        sums_ref[...] = jnp.zeros_like(sums_ref)
    for copy in parts:
        copy.wait()
    if with_ones:
        sub = lax.broadcasted_iota(jnp.int32, (rows, width), 0)
        for begin in (0, reach + count_tiles):

            def fix(k, carry, begin=begin):
                value = window[begin + k].astype(F32)
                window[begin + k] = jnp.where(sub == channels + 2, 1.0, value).astype(BF16)
                return carry

            lax.fori_loop(0, reach, fix, 0, unroll=4)
    stores = Loads([(result, out_ref, 0)], BAND_LOADS, out_sems, 0)
    for load in range(BAND_LOADS):
        loads.start(load + AHEAD)
        loads.wait(load)

        def tile(k, carry, load=load):
            t = load * here + k
            places = [t + offsets_ref[t * band + b] + reach for b in range(band)]
            matrices = [weights[t, b] for b in range(band)]
            sources = jnp.concatenate([window[place] for place in places], axis=1)
            mixed = product(sources, jnp.concatenate(matrices, axis=1))
            known = [ts[:, pl.ds(pl.multiple_of(t * width, width), width)]]
            known.append(rows8({2: counts_ref[pl.ds(t, 1), :].astype(F32)}))
            result[t] = mixed + jnp.concatenate(known, axis=0)
            if with_ones:
                for place, matrix in zip(places, matrices):
                    sums_ref[pl.ds(place, 1), :] += jnp.sum(matrix.astype(F32), axis=0, keepdims=True)
            return carry

        lax.fori_loop(0, here, tile, 0, unroll=4)
        stores.start(load)
    for load in range(BAND_LOADS):
        stores.wait(load)


def add_remote(landing_ref, in_ref, weights_ref, band_ref, incoming, weights, band, acc, sems, each=None, small=()):
    shards, rows, width = incoming.shape
    group = shards // LOADS
    loads = Loads([(in_ref, incoming, 0), (weights_ref, weights, 0)], LOADS, sems, 0)
    band_loads = Loads([(band_ref, band, 0)], PARTS, sems, 2 * LOADS)
    for load in range(AHEAD):
        loads.start(load)
    for load in small:
        load.start()

    def clear(t, carry):
        acc[t] = jnp.zeros((rows, width), F32)
        return carry

    lax.fori_loop(0, acc.shape[0], clear, 0, unroll=8)
    for load in small:
        load.wait()
    seen = jnp.zeros((EXTRA, width), F32)
    for load in range(LOADS):
        loads.start(load + AHEAD)
        if load + AHEAD >= LOADS:
            band_loads.start(load + AHEAD - LOADS)
        loads.wait(load)

        def pair(k, seen, load=load):
            p = load * group + 2 * k
            values = [incoming[p], incoming[p + 1]]
            tails = [value.astype(F32)[rows - EXTRA :] for value in values]
            mixed = two_products(values, [weights[p], weights[p + 1]])
            for i in range(2):
                acc[landing_ref[p + i]] += mixed[i]
                if each is not None:
                    each(p + i, tails[i])
            return seen + (tails[0] + tails[1])

        seen = lax.fori_loop(0, group // 2, pair, seen, unroll=8)
    for part in range(AHEAD, PARTS):
        band_loads.start(part)
    return seen, band_loads


def first_kernel(
    odd_ref, send_ref, landing_ref, in_ref, weights_ref, band_ref, columns_ref,
    inner_ref, outer_ref, out_ref, recip_ref, first_ref,
    incoming, weights, band, acc, tiles, columns, recips, firsts, messages, sems, out_sems,
):
    shards, rows, width = incoming.shape
    channels = rows - EXTRA
    count_tiles = acc.shape[0]
    half = count_tiles // 2
    column_load = pltpu.make_async_copy(columns_ref, columns, out_sems.at[0])

    def each(p, tail):
        columns[pl.ds(send_ref[p], 1), :] += tail[6:7] + tail[7:8]

    seen, band_loads = add_remote(
        landing_ref, in_ref, weights_ref, band_ref, incoming, weights, band, acc, sems, each, [column_load]
    )
    known = seen[3:4, :] + seen[4:5, :] + seen[5:6, :]
    count_total = pick_lane(known, channels)
    first = jnp.broadcast_to(PRIOR * to_column(known, channels) / count_total, (channels, width))
    firsts[...] = jnp.broadcast_to(known, firsts.shape)
    zero = jnp.zeros((channels, width), F32)
    line = jnp.zeros((1, width), F32)
    carry = (zero, zero, line, line)
    stores = []
    halves = Halves(odd_ref[0], tiles, half, inner_ref, outer_ref, out_sems, 3, PARTS)
    part = count_tiles // PARTS
    for number in range(PARTS):
        band_loads.wait(number)

        def finish(k, carry, number=number):
            t = number * part + k
            all_totals, all_states, all_weights, all_recips = carry
            mixed = acc[t] + band[t]
            spread = mixed[channels : channels + 1] + mixed[channels + 1 : channels + 2]
            totals = mixed[:channels] + first * spread
            weight = mixed[channels + 2 : channels + 3]
            recip = 1.0 / (weight + PRIOR)
            recips[pl.ds(t, 1), :] = recip
            high, low = pieces(recip, 2)
            state = (totals * recip).astype(BF16).astype(F32)
            tiles[t] = stacked(state, rows8({0: high, 1: low}))
            column = columns[pl.ds(t, 1), :]
            return (
                all_totals + totals,
                all_states + state * column,
                all_weights + weight,
                all_recips + (high + low) * column,
            )

        carry = lax.fori_loop(0, part, finish, carry, unroll=4)
        halves.start(number)
    all_totals, all_states, all_weights, all_recips = carry
    row = to_row(jnp.sum(all_totals, axis=1, keepdims=True))
    row = row + to_row(jnp.sum(all_states, axis=1, keepdims=True), channels)
    scalars = at_lane(total(all_weights), 0) + at_lane(total(all_recips), 1)
    one, two, three = pieces(row, 3)
    uno, due, tre = pieces(scalars, 3)
    block = rows8({2: uno, 3: one, 4: two, 5: three, 6: due, 7: tre})
    for source, ref in ((recips, recip_ref), (firsts, first_ref)):
        stores.append(pltpu.make_async_copy(source, ref, out_sems.at[len(stores)]))
        stores[-1].start()
    messages_out = store_messages(send_ref, tiles, messages, out_ref, out_sems, 3 + PARTS, block)
    for store in stores:
        store.wait()
    for number in range(PARTS):
        halves.wait(number)
    for number in range(MESSAGE_PARTS):
        messages_out.wait(number)


def last_kernel(
    landing_ref, in_ref, weights_ref, band_ref, recip_ref, first_ref, out_ref,
    incoming, weights, band, acc, result, recips, firsts, sems, out_sems,
):
    shards, rows, width = incoming.shape
    channels = rows - EXTRA
    count_tiles = acc.shape[0]
    small = [
        pltpu.make_async_copy(recip_ref, recips, out_sems.at[0]),
        pltpu.make_async_copy(first_ref, firsts, out_sems.at[1]),
    ]
    seen, band_loads = add_remote(
        landing_ref, in_ref, weights_ref, band_ref, incoming, weights, band, acc, sems, None, small
    )
    known = seen[3:4, :] + seen[4:5, :] + seen[5:6, :]
    scalars = seen[2:3, :] + seen[6:7, :] + seen[7:8, :]
    weight_total, spread_total = pick_lane(scalars, 0), pick_lane(scalars, 1)
    mean = PRIOR * to_column(known, channels) / weight_total
    mixed_total = to_column(known, channels, channels) + mean * spread_total
    last = PRIOR * (to_column(firsts[0:1, :], channels) + mixed_total) / weight_total
    mean, last = jnp.broadcast_to(mean, (channels, width)), jnp.broadcast_to(last, (channels, width))
    stores = []
    part = count_tiles // PARTS
    for number in range(PARTS):
        band_loads.wait(number)

        def finish(k, carry, number=number):
            t = number * part + k
            mixed = acc[t] + band[t]
            spread = mixed[channels : channels + 1] + mixed[channels + 1 : channels + 2]
            at = pl.ds(pl.multiple_of(t * width, width), width)
            result[:, at] = (mixed[:channels] + mean * spread + last) * recips[pl.ds(t, 1), :]
            return carry

        lax.fori_loop(0, part, finish, 0, unroll=4)
        at = pl.ds(number * part * width, part * width)
        stores.append(pltpu.make_async_copy(result.at[:, at], out_ref.at[:, at], out_sems.at[number]))
        stores[-1].start()
    for store in stores:
        store.wait()


def params(mib):
    return pltpu.CompilerParams(vmem_limit_bytes=mib * 2**20)


def cost(flops, size):
    return pl.CostEstimate(flops=flops, bytes_accessed=size, transcendentals=0)


def whole(shape):
    zeros = (0,) * len(shape)
    return pl.BlockSpec(shape, lambda *_: zeros)


ANY = pl.BlockSpec(memory_space=pl.ANY)


def shapes(count_tiles, rows, shards, width=128):
    tile = jax.ShapeDtypeStruct((count_tiles // 2, rows, width), BF16)
    message = jax.ShapeDtypeStruct((shards, rows, width), BF16)
    return tile, message


def call(kernel, prefetch, in_specs, out_specs, out_shape, scratch, name, estimate, limit=VMEM):
    return pl.pallas_call(
        kernel,
        grid_spec=pltpu.PrefetchScalarGridSpec(
            num_scalar_prefetch=prefetch,
            grid=(1,),
            in_specs=in_specs,
            out_specs=out_specs,
            scratch_shapes=scratch,
        ),
        out_shape=out_shape,
        compiler_params=params(limit),
        cost_estimate=estimate,
        name=name,
    )


def sems(count):
    return pltpu.SemaphoreType.DMA((count,))


def prep(odd, send, ts, counts, remote_weights):
    channels, columns = ts.shape
    count_tiles, width = counts.shape
    rows = channels + EXTRA
    tile, message = shapes(count_tiles, rows, send.shape[0])
    scratch = [
        pltpu.VMEM(ts.shape, F32),
        pltpu.VMEM(counts.shape, jnp.int32),
        pltpu.VMEM(remote_weights.shape, BF16),
        pltpu.VMEM((count_tiles, rows, width), BF16),
        pltpu.VMEM(message.shape, BF16),
        sems(LOADS + 1 + MESSAGE_PARTS),
        sems(PARTS + MESSAGE_PARTS),
    ]
    return call(
        prep_kernel, 2, [ANY] * 3, [ANY] * 3, [tile, tile, message], scratch, "prep", cost(10**6, 5 * 10**6)
    )(odd, send, ts, counts, remote_weights)


def band_product(with_ones, odd, offsets, ts, counts, inner, outer, from_inner, from_outer, band_weights):
    count_tiles, _, width, _ = band_weights.shape
    rows = inner.shape[1]
    shape = (count_tiles, rows, width)
    scratch = [
        pltpu.VMEM(ts.shape, F32),
        pltpu.VMEM(band_weights.shape, BF16),
        pltpu.VMEM((2 * count_tiles, rows, width), BF16),
        pltpu.VMEM(shape, F32),
        sems(2 * BAND_LOADS + 4),
        sems(BAND_LOADS),
    ]
    out_shape, out_specs = [jax.ShapeDtypeStruct(shape, F32)], [ANY]
    if with_ones:
        out_shape.append(jax.ShapeDtypeStruct((2 * count_tiles, width), F32))
        out_specs.append(whole(out_shape[1].shape))
    return call(
        functools.partial(band_kernel, with_ones), 2, [ANY, whole(counts.shape)] + [ANY] * 5, out_specs,
        out_shape, scratch, "band", cost(BAND_COST, 20 * 10**6), VMEM_BAND,
    )(odd, offsets, ts, counts, inner, outer, from_inner, from_outer, band_weights)


def round_scratch(incoming, remote_weights, mixed):
    return [
        pltpu.VMEM(incoming.shape, BF16),
        pltpu.VMEM(remote_weights.shape, BF16),
        pltpu.VMEM(mixed.shape, F32),
        pltpu.VMEM(mixed.shape, F32),
    ]


def first_round(odd, send, landing, incoming, remote_weights, mixed, columns):
    shards, rows, width = incoming.shape
    count_tiles = mixed.shape[0]
    tile, message = shapes(count_tiles, rows, shards)
    recip = jax.ShapeDtypeStruct((count_tiles, width), F32)
    first = jax.ShapeDtypeStruct((8, width), F32)
    scratch = round_scratch(incoming, remote_weights, mixed) + [
        pltpu.VMEM(mixed.shape, BF16),
        pltpu.VMEM(columns.shape, F32),
        pltpu.VMEM(recip.shape, F32),
        pltpu.VMEM(first.shape, F32),
        pltpu.VMEM(message.shape, BF16),
        sems(PARTS + 2 * LOADS),
        sems(3 + PARTS + MESSAGE_PARTS),
    ]
    return call(
        first_kernel, 3, [ANY] * 4, [ANY] * 5, [tile, tile, message, recip, first], scratch, "first",
        cost(2 * 128 * 72 * 128 * 128, 20 * 10**6), VMEM_ROUND,
    )(odd, send, landing, incoming, remote_weights, mixed, columns)


def last_round(landing, incoming, remote_weights, mixed, recip, first):
    rows, width = incoming.shape[1:]
    shape = (rows - EXTRA, mixed.shape[0] * width)
    scratch = round_scratch(incoming, remote_weights, mixed) + [
        pltpu.VMEM(shape, F32),
        pltpu.VMEM(recip.shape, F32),
        pltpu.VMEM(first.shape, F32),
        sems(PARTS + 2 * LOADS),
        sems(PARTS),
    ]
    return call(
        last_kernel, 1, [ANY] * 5, ANY, jax.ShapeDtypeStruct(shape, F32), scratch, "last",
        cost(2 * 128 * 72 * 128 * 128, 20 * 10**6), VMEM_ROUND,
    )(landing, incoming, remote_weights, mixed, recip, first)


def on_device(target_sums, counts, band_offsets, band_weights, send_tiles, landing_tiles, remote_weights):
    count_tiles, _, width, _ = band_weights.shape
    shards = remote_weights.shape[0]
    reach = count_tiles // 2
    counts = counts.reshape(count_tiles, width)
    send, landing, offsets = send_tiles.reshape(-1), landing_tiles.reshape(-1), band_offsets.reshape(-1)
    parity = lax.axis_index("item") % 2
    odd = parity.reshape(1)
    inner_pairs = [(i, i ^ 1) for i in range(shards)]
    outer_pairs = [(i, i + 1 if i % 2 else i - 1) for i in range(1, shards - 1)]

    def swap(inner, outer):
        return lax.ppermute(inner, "item", inner_pairs), lax.ppermute(outer, "item", outer_pairs)

    def exchange(inner, outer, outgoing):
        halo = swap(inner, outer)
        return halo, lax.all_to_all(outgoing, "item", split_axis=0, concat_axis=0, tiled=True)

    inner, outer, outgoing = prep(odd, send, target_sums, counts, remote_weights)
    halo, incoming = exchange(inner, outer, outgoing)
    mixed, sums = band_product(True, odd, offsets, target_sums, counts, inner, outer, *halo, band_weights)
    below, above = sums[:reach], sums[reach + count_tiles :]
    from_inner, from_outer = swap(
        jnp.where(parity == 1, below, above), jnp.where(parity == 1, above, below)
    )
    lower, upper = (
        jnp.where(parity == 1, from_inner, from_outer), jnp.where(parity == 1, from_outer, from_inner)
    )
    columns = sums[reach : reach + count_tiles] + jnp.concatenate([lower, upper], axis=0)
    inner, outer, outgoing, recip, first = first_round(
        odd, send, landing, incoming, remote_weights, mixed, columns
    )
    halo, incoming = exchange(inner, outer, outgoing)
    (mixed,) = band_product(False, odd, offsets, target_sums, counts, inner, outer, *halo, band_weights)
    return last_round(landing, incoming, remote_weights, mixed, recip, first)


def solution(mesh):
    return jax.shard_map(
        on_device,
        mesh=mesh,
        in_specs=(
            P(None, "item"),
            P("item"),
            P("item", None),
            P("item", None, None, None),
            P("item", None),
            P("item", None),
            P("item", None, None),
        ),
        out_specs=P(None, "item"),
        check_vma=False,
    )
```

```python
import functools

import jax
import jax.numpy as jnp
from jax import lax
from jax.experimental import pallas as pl
from jax.experimental.pallas import tpu as pltpu
from jax.sharding import PartitionSpec as P

PRIOR = 20.0
EXTRA = 8
F32 = jnp.float32
BF16 = jnp.bfloat16
LOADS = 8
BAND_LOADS = 12
PARTS = 4
MESSAGE_PARTS = 8
BAND_COST = 10**11
MESSAGE_COST = 10**6
VMEM = 60
VMEM_ROUND = 60
VMEM_BAND = 52
AHEAD = 5


def pieces(value, count):
    parts = []
    for _ in range(count):
        part = value.astype(BF16).astype(F32)
        parts.append(part)
        value = value - part
    return parts


def rows8(rows, base=None):
    width = 128
    index = lax.broadcasted_iota(jnp.int32, (EXTRA, width), 0)
    block = jnp.zeros((EXTRA, width), F32) if base is None else base
    for place, row in rows.items():
        block = jnp.where(index == place, row, block)
    return block


def to_row(column, shift=0):
    channels = column.shape[0]
    lane = lax.broadcasted_iota(jnp.int32, (channels, 128), 1)
    sub = lax.broadcasted_iota(jnp.int32, (channels, 128), 0)
    return jnp.sum(jnp.where(lane == sub + shift, column, 0.0), axis=0, keepdims=True)


def to_column(row, channels, shift=0):
    lane = lax.broadcasted_iota(jnp.int32, (channels, 128), 1)
    sub = lax.broadcasted_iota(jnp.int32, (channels, 128), 0)
    return jnp.sum(jnp.where(lane == sub + shift, row, 0.0), axis=1, keepdims=True)


def at_lane(scalar, place):
    lane = lax.broadcasted_iota(jnp.int32, (1, 128), 1)
    return jnp.where(lane == place, scalar, 0.0)


def pick_lane(row, place):
    lane = lax.broadcasted_iota(jnp.int32, (1, 128), 1)
    return jnp.sum(jnp.where(lane == place, row, 0.0), axis=1, keepdims=True)


def total(block):
    return jnp.sum(jnp.sum(block, axis=0, keepdims=True), axis=1, keepdims=True)


def stacked(top, bottom):
    return jnp.concatenate([top, bottom], axis=0).astype(BF16)


def product(tile, weights):
    return lax.dot_general(tile, weights, (((1,), (1,)), ((), ())), preferred_element_type=F32)


class Loads:
    def __init__(self, pairs, count, sems, first):
        self.parts, self.count = [], count
        for i in range(count):
            part = []
            for number, (source, target, axis) in enumerate(pairs):
                size = source.shape[axis] // count
                at = (slice(None),) * axis + (pl.ds(i * size, size),)
                sem = sems.at[first + i * len(pairs) + number]
                part.append(pltpu.make_async_copy(source.at[at], target.at[at], sem))
            self.parts.append(part)

    def start(self, i):
        if i < self.count:
            for copy in self.parts[i]:
                copy.start()

    def wait(self, i):
        for copy in self.parts[i]:
            copy.wait()


def two_products(tiles, weights):
    rows, width = tiles[0].shape
    both = product(jnp.concatenate(tiles, axis=0), jnp.concatenate(weights, axis=0))
    return both[:rows, :width], both[rows:, width:]


class Halves:
    def __init__(self, odd, tiles, half, inner_ref, outer_ref, sems, first, parts):
        self.odd, self.copies, size = odd, [], half // (parts // 2)
        for i in range(parts):
            source, at = tiles.at[pl.ds(i * size, size)], pl.ds(i * size % half, size)
            inner = pltpu.make_async_copy(source, inner_ref.at[at], sems.at[first + i])
            outer = pltpu.make_async_copy(source, outer_ref.at[at], sems.at[first + i])
            upper = i >= parts // 2
            self.copies.append((outer, inner) if upper else (inner, outer))

    def start(self, i):
        pl.when(self.odd == 1)(self.copies[i][0].start)
        pl.when(self.odd == 0)(self.copies[i][1].start)

    def wait(self, i):
        pl.when(self.odd == 1)(self.copies[i][0].wait)
        pl.when(self.odd == 0)(self.copies[i][1].wait)


def message_kernel(with_columns, odd_ref, send_ref, inner_ref, outer_ref, block_ref, *rest):
    if with_columns:
        remote_ref, out_ref, tiles, messages, block, sems, out_sems, remote, columns = rest
    else:
        out_ref, tiles, messages, block, sems, out_sems = rest
    count, rows, width = messages.shape
    half = inner_ref.shape[0]
    odd = odd_ref[0]
    loads = [
        pltpu.make_async_copy(inner_ref, tiles.at[pl.ds((1 - odd) * half, half)], sems.at[0]),
        pltpu.make_async_copy(outer_ref, tiles.at[pl.ds(odd * half, half)], sems.at[1]),
        pltpu.make_async_copy(block_ref, block, sems.at[2]),
    ]
    for load in loads:
        load.start()
    top = jnp.zeros((rows - EXTRA, width), F32)
    part = count // MESSAGE_PARTS
    if with_columns:
        remote_loads = Loads([(remote_ref, remote, 0)], MESSAGE_PARTS, sems, 3)
        for i in range(MESSAGE_PARTS):
            remote_loads.start(i)
    for load in loads:
        load.wait()
    shared = block[...]
    stores = Loads([(messages, out_ref, 0)], MESSAGE_PARTS, out_sems, 0)
    for number in range(MESSAGE_PARTS):
        if with_columns:
            remote_loads.wait(number)

            def column(k, carry, number=number):
                q = number * part + k
                columns[pl.ds(q, 1), :] = jnp.sum(remote[q].astype(F32), axis=0, keepdims=True)
                return carry

            lax.fori_loop(0, part, column, 0, unroll=8)

        def step(k, carry, number=number):
            q = number * part + k
            extra = shared
            if with_columns:
                high, low = pieces(columns[pl.ds(q, 1), :], 2)
                extra = rows8({6: high, 7: low}, shared)
            messages[q] = tiles[send_ref[q]] + stacked(top, extra)
            return carry

        lax.fori_loop(0, part, step, 0, unroll=8)
        stores.start(number)
    for number in range(MESSAGE_PARTS):
        stores.wait(number)


def prep_kernel(
    odd_ref, ts_ref, counts_ref, inner_ref, outer_ref, block_ref, ts, counts, tiles, block, sems, out_sems
):
    channels, width = ts.shape[0], counts.shape[1]
    count_tiles = tiles.shape[0]
    half = count_tiles // 2
    here = count_tiles // LOADS
    loads = Loads([(ts_ref, ts, 1)], LOADS, sems, 0)
    count_load = pltpu.make_async_copy(counts_ref, counts, sems.at[LOADS])
    count_load.start()
    for load in range(LOADS):
        loads.start(load)
    stores = Halves(odd_ref[0], tiles, half, inner_ref, outer_ref, out_sems, 0, PARTS)
    count_load.wait()
    part = jnp.zeros((channels, width), F32)
    for load in range(LOADS):
        loads.wait(load)

        def tile(k, part, load=load):
            t = load * here + k
            values = ts[:, pl.ds(pl.multiple_of(t * width, width), width)]
            count = counts[pl.ds(t, 1), :].astype(F32)
            recip = 1.0 / (count + PRIOR)
            high, low = pieces(recip, 2)
            tiles[t] = stacked(values * recip, rows8({0: high, 1: low, 2: jnp.ones_like(recip)}))
            return part + values

        part = lax.fori_loop(0, here, tile, part, unroll=4)
        if (load + 1) % (LOADS // PARTS) == 0:
            stores.start(load // (LOADS // PARTS))
    row = to_row(jnp.sum(part, axis=1, keepdims=True))
    row = row + at_lane(total(counts[...].astype(F32)), channels)
    one, two, three = pieces(row, 3)
    block[...] = rows8({3: one, 4: two, 5: three})
    block_store = pltpu.make_async_copy(block, block_ref, sems.at[LOADS])
    block_store.start()
    block_store.wait()
    for i in range(PARTS):
        stores.wait(i)


def band_kernel(
    with_ones, odd_ref, offsets_ref, ts_ref, counts_ref, inner_ref, outer_ref, from_inner_ref, from_outer_ref,
    weights_ref, out_ref, *rest
):
    if with_ones:
        sums_ref, ts, weights, window, result, sems, out_sems = rest
    else:
        ts, weights, window, result, sems, out_sems = rest
    count_tiles, band = weights.shape[:2]
    reach, rows, width = inner_ref.shape
    channels = rows - EXTRA
    here = count_tiles // BAND_LOADS
    odd = odd_ref[0]
    parts = []
    for i, (ref, at) in enumerate(
        ((inner_ref, 2 - odd), (outer_ref, 1 + odd), (from_inner_ref, 3 - 3 * odd), (from_outer_ref, 3 * odd))
    ):
        copy = pltpu.make_async_copy(ref, window.at[pl.ds(at * reach, reach)], sems.at[2 * BAND_LOADS + i])
        copy.start()
        parts.append(copy)
    loads = Loads([(weights_ref, weights, 0), (ts_ref, ts, 1)], BAND_LOADS, sems, 0)
    for load in range(AHEAD):
        loads.start(load)
    if with_ones:
        sums_ref[...] = jnp.zeros_like(sums_ref)
    for copy in parts:
        copy.wait()
    if with_ones:
        sub = lax.broadcasted_iota(jnp.int32, (rows, width), 0)
        for begin in (0, reach + count_tiles):

            def fix(k, carry, begin=begin):
                value = window[begin + k].astype(F32)
                window[begin + k] = jnp.where(sub == channels + 2, 1.0, value).astype(BF16)
                return carry

            lax.fori_loop(0, reach, fix, 0, unroll=4)
    stores = Loads([(result, out_ref, 0)], BAND_LOADS, out_sems, 0)
    for load in range(BAND_LOADS):
        loads.start(load + AHEAD)
        loads.wait(load)

        def tile(k, carry, load=load):
            t = load * here + k
            places = [t + offsets_ref[t * band + b] + reach for b in range(band)]
            matrices = [weights[t, b] for b in range(band)]
            sources = jnp.concatenate([window[place] for place in places], axis=1)
            mixed = product(sources, jnp.concatenate(matrices, axis=1))
            known = [ts[:, pl.ds(pl.multiple_of(t * width, width), width)]]
            known.append(rows8({2: counts_ref[pl.ds(t, 1), :].astype(F32)}))
            result[t] = mixed + jnp.concatenate(known, axis=0)
            if with_ones:
                for place, matrix in zip(places, matrices):
                    sums_ref[pl.ds(place, 1), :] += jnp.sum(matrix.astype(F32), axis=0, keepdims=True)
            return carry

        lax.fori_loop(0, here, tile, 0, unroll=4)
        stores.start(load)
    for load in range(BAND_LOADS):
        stores.wait(load)


def add_remote(landing_ref, in_ref, weights_ref, band_ref, incoming, weights, band, acc, sems, each=None, small=()):
    shards, rows, width = incoming.shape
    group = shards // LOADS
    loads = Loads([(in_ref, incoming, 0), (weights_ref, weights, 0)], LOADS, sems, 0)
    band_loads = Loads([(band_ref, band, 0)], PARTS, sems, 2 * LOADS)
    for load in range(AHEAD):
        loads.start(load)
    for load in small:
        load.start()

    def clear(t, carry):
        acc[t] = jnp.zeros((rows, width), F32)
        return carry

    lax.fori_loop(0, acc.shape[0], clear, 0, unroll=8)
    for load in small:
        load.wait()
    seen = jnp.zeros((EXTRA, width), F32)
    for load in range(LOADS):
        loads.start(load + AHEAD)
        if load + AHEAD >= LOADS:
            band_loads.start(load + AHEAD - LOADS)
        loads.wait(load)

        def pair(k, seen, load=load):
            p = load * group + 2 * k
            values = [incoming[p], incoming[p + 1]]
            tails = [value.astype(F32)[rows - EXTRA :] for value in values]
            mixed = two_products(values, [weights[p], weights[p + 1]])
            for i in range(2):
                acc[landing_ref[p + i]] += mixed[i]
                if each is not None:
                    each(p + i, tails[i])
            return seen + (tails[0] + tails[1])

        seen = lax.fori_loop(0, group // 2, pair, seen, unroll=8)
    for part in range(AHEAD, PARTS):
        band_loads.start(part)
    return seen, band_loads


def first_kernel(
    odd_ref, send_ref, landing_ref, in_ref, weights_ref, band_ref, columns_ref,
    inner_ref, outer_ref, block_ref, recip_ref, first_ref,
    incoming, weights, band, acc, tiles, columns, recips, firsts, block, sems, out_sems,
):
    shards, rows, width = incoming.shape
    channels = rows - EXTRA
    count_tiles = acc.shape[0]
    half = count_tiles // 2
    column_load = pltpu.make_async_copy(columns_ref, columns, out_sems.at[0])

    def each(p, tail):
        columns[pl.ds(send_ref[p], 1), :] += tail[6:7] + tail[7:8]

    seen, band_loads = add_remote(
        landing_ref, in_ref, weights_ref, band_ref, incoming, weights, band, acc, sems, each, [column_load]
    )
    known = seen[3:4, :] + seen[4:5, :] + seen[5:6, :]
    count_total = pick_lane(known, channels)
    first = jnp.broadcast_to(PRIOR * to_column(known, channels) / count_total, (channels, width))
    firsts[...] = jnp.broadcast_to(known, firsts.shape)
    zero = jnp.zeros((channels, width), F32)
    line = jnp.zeros((1, width), F32)
    carry = (zero, zero, line, line)
    stores = []
    halves = Halves(odd_ref[0], tiles, half, inner_ref, outer_ref, out_sems, 3, PARTS)
    part = count_tiles // PARTS
    for number in range(PARTS):
        band_loads.wait(number)

        def finish(k, carry, number=number):
            t = number * part + k
            all_totals, all_states, all_weights, all_recips = carry
            mixed = acc[t] + band[t]
            spread = mixed[channels : channels + 1] + mixed[channels + 1 : channels + 2]
            totals = mixed[:channels] + first * spread
            weight = mixed[channels + 2 : channels + 3]
            recip = 1.0 / (weight + PRIOR)
            recips[pl.ds(t, 1), :] = recip
            high, low = pieces(recip, 2)
            state = (totals * recip).astype(BF16).astype(F32)
            tiles[t] = stacked(state, rows8({0: high, 1: low}))
            column = columns[pl.ds(t, 1), :]
            return (
                all_totals + totals,
                all_states + state * column,
                all_weights + weight,
                all_recips + (high + low) * column,
            )

        carry = lax.fori_loop(0, part, finish, carry, unroll=4)
        halves.start(number)
    all_totals, all_states, all_weights, all_recips = carry
    row = to_row(jnp.sum(all_totals, axis=1, keepdims=True))
    row = row + to_row(jnp.sum(all_states, axis=1, keepdims=True), channels)
    scalars = at_lane(total(all_weights), 0) + at_lane(total(all_recips), 1)
    one, two, three = pieces(row, 3)
    uno, due, tre = pieces(scalars, 3)
    block[...] = rows8({2: uno, 3: one, 4: two, 5: three, 6: due, 7: tre})
    for source, ref in ((recips, recip_ref), (firsts, first_ref), (block, block_ref)):
        stores.append(pltpu.make_async_copy(source, ref, out_sems.at[len(stores)]))
        stores[-1].start()
    for store in stores:
        store.wait()
    for number in range(PARTS):
        halves.wait(number)


def last_kernel(
    landing_ref, in_ref, weights_ref, band_ref, recip_ref, first_ref, out_ref,
    incoming, weights, band, acc, result, recips, firsts, sems, out_sems,
):
    shards, rows, width = incoming.shape
    channels = rows - EXTRA
    count_tiles = acc.shape[0]
    small = [
        pltpu.make_async_copy(recip_ref, recips, out_sems.at[0]),
        pltpu.make_async_copy(first_ref, firsts, out_sems.at[1]),
    ]
    seen, band_loads = add_remote(
        landing_ref, in_ref, weights_ref, band_ref, incoming, weights, band, acc, sems, None, small
    )
    known = seen[3:4, :] + seen[4:5, :] + seen[5:6, :]
    scalars = seen[2:3, :] + seen[6:7, :] + seen[7:8, :]
    weight_total, spread_total = pick_lane(scalars, 0), pick_lane(scalars, 1)
    mean = PRIOR * to_column(known, channels) / weight_total
    mixed_total = to_column(known, channels, channels) + mean * spread_total
    last = PRIOR * (to_column(firsts[0:1, :], channels) + mixed_total) / weight_total
    mean, last = jnp.broadcast_to(mean, (channels, width)), jnp.broadcast_to(last, (channels, width))
    stores = []
    part = count_tiles // PARTS
    for number in range(PARTS):
        band_loads.wait(number)

        def finish(k, carry, number=number):
            t = number * part + k
            mixed = acc[t] + band[t]
            spread = mixed[channels : channels + 1] + mixed[channels + 1 : channels + 2]
            at = pl.ds(pl.multiple_of(t * width, width), width)
            result[:, at] = (mixed[:channels] + mean * spread + last) * recips[pl.ds(t, 1), :]
            return carry

        lax.fori_loop(0, part, finish, 0, unroll=4)
        at = pl.ds(number * part * width, part * width)
        stores.append(pltpu.make_async_copy(result.at[:, at], out_ref.at[:, at], out_sems.at[number]))
        stores[-1].start()
    for store in stores:
        store.wait()


def params(mib):
    return pltpu.CompilerParams(vmem_limit_bytes=mib * 2**20)


def cost(flops, size):
    return pl.CostEstimate(flops=flops, bytes_accessed=size, transcendentals=0)


def whole(shape):
    zeros = (0,) * len(shape)
    return pl.BlockSpec(shape, lambda *_: zeros)


ANY = pl.BlockSpec(memory_space=pl.ANY)


def shapes(count_tiles, rows, shards, width=128):
    tile = jax.ShapeDtypeStruct((count_tiles // 2, rows, width), BF16)
    message = jax.ShapeDtypeStruct((shards, rows, width), BF16)
    return tile, message


def call(kernel, prefetch, in_specs, out_specs, out_shape, scratch, name, estimate, limit=VMEM):
    return pl.pallas_call(
        kernel,
        grid_spec=pltpu.PrefetchScalarGridSpec(
            num_scalar_prefetch=prefetch,
            grid=(1,),
            in_specs=in_specs,
            out_specs=out_specs,
            scratch_shapes=scratch,
        ),
        out_shape=out_shape,
        compiler_params=params(limit),
        cost_estimate=estimate,
        name=name,
    )


def sems(count):
    return pltpu.SemaphoreType.DMA((count,))


def prep(odd, ts, counts, shards):
    channels, columns = ts.shape
    count_tiles, width = counts.shape
    rows = channels + EXTRA
    tile, _ = shapes(count_tiles, rows, shards)
    block = jax.ShapeDtypeStruct((EXTRA, width), F32)
    scratch = [
        pltpu.VMEM(ts.shape, F32),
        pltpu.VMEM(counts.shape, jnp.int32),
        pltpu.VMEM((count_tiles, rows, width), BF16),
        pltpu.VMEM(block.shape, F32),
        sems(LOADS + 1),
        sems(PARTS),
    ]
    return call(
        prep_kernel, 1, [ANY] * 2, [ANY] * 3, [tile, tile, block], scratch,
        "prep", cost(10**6, 5 * 10**6),
    )(odd, ts, counts)


def fill_messages(odd, send, inner, outer, block, remote_weights=None):
    half, rows, width = inner.shape
    shards = send.shape[0]
    _, message = shapes(2 * half, rows, shards)
    scratch = [
        pltpu.VMEM((2 * half, rows, width), BF16),
        pltpu.VMEM(message.shape, BF16),
        pltpu.VMEM(block.shape, F32),
        sems(3 + MESSAGE_PARTS),
        sems(MESSAGE_PARTS),
    ]
    operands = [odd, send, inner, outer, block]
    if remote_weights is not None:
        operands.append(remote_weights)
        scratch += [pltpu.VMEM(remote_weights.shape, BF16), pltpu.VMEM((shards, width), F32)]
    return call(
        functools.partial(message_kernel, remote_weights is not None), 2, [ANY] * (len(operands) - 2), ANY,
        message, scratch, "messages", cost(MESSAGE_COST, 5 * 10**6),
    )(*operands)


def band_product(with_ones, odd, offsets, ts, counts, inner, outer, from_inner, from_outer, band_weights):
    count_tiles, _, width, _ = band_weights.shape
    rows = inner.shape[1]
    shape = (count_tiles, rows, width)
    scratch = [
        pltpu.VMEM(ts.shape, F32),
        pltpu.VMEM(band_weights.shape, BF16),
        pltpu.VMEM((2 * count_tiles, rows, width), BF16),
        pltpu.VMEM(shape, F32),
        sems(2 * BAND_LOADS + 4),
        sems(BAND_LOADS),
    ]
    out_shape, out_specs = [jax.ShapeDtypeStruct(shape, F32)], [ANY]
    if with_ones:
        out_shape.append(jax.ShapeDtypeStruct((2 * count_tiles, width), F32))
        out_specs.append(whole(out_shape[1].shape))
    return call(
        functools.partial(band_kernel, with_ones), 2, [ANY, whole(counts.shape)] + [ANY] * 5, out_specs,
        out_shape, scratch, "band", cost(BAND_COST, 20 * 10**6), VMEM_BAND,
    )(odd, offsets, ts, counts, inner, outer, from_inner, from_outer, band_weights)


def round_scratch(incoming, remote_weights, mixed):
    return [
        pltpu.VMEM(incoming.shape, BF16),
        pltpu.VMEM(remote_weights.shape, BF16),
        pltpu.VMEM(mixed.shape, F32),
        pltpu.VMEM(mixed.shape, F32),
    ]


def first_round(odd, send, landing, incoming, remote_weights, mixed, columns):
    shards, rows, width = incoming.shape
    count_tiles = mixed.shape[0]
    tile, _ = shapes(count_tiles, rows, shards)
    recip = jax.ShapeDtypeStruct((count_tiles, width), F32)
    first = jax.ShapeDtypeStruct((8, width), F32)
    scratch = round_scratch(incoming, remote_weights, mixed) + [
        pltpu.VMEM(mixed.shape, BF16),
        pltpu.VMEM(columns.shape, F32),
        pltpu.VMEM(recip.shape, F32),
        pltpu.VMEM(first.shape, F32),
        pltpu.VMEM((EXTRA, width), F32),
        sems(PARTS + 2 * LOADS),
        sems(3 + PARTS),
    ]
    return call(
        first_kernel, 3, [ANY] * 4, [ANY] * 5, [tile, tile, first, recip, first], scratch, "first",
        cost(2 * 128 * 72 * 128 * 128, 20 * 10**6), VMEM_ROUND,
    )(odd, send, landing, incoming, remote_weights, mixed, columns)


def last_round(landing, incoming, remote_weights, mixed, recip, first):
    rows, width = incoming.shape[1:]
    shape = (rows - EXTRA, mixed.shape[0] * width)
    scratch = round_scratch(incoming, remote_weights, mixed) + [
        pltpu.VMEM(shape, F32),
        pltpu.VMEM(recip.shape, F32),
        pltpu.VMEM(first.shape, F32),
        sems(PARTS + 2 * LOADS),
        sems(PARTS),
    ]
    return call(
        last_kernel, 1, [ANY] * 5, ANY, jax.ShapeDtypeStruct(shape, F32), scratch, "last",
        cost(2 * 128 * 72 * 128 * 128, 20 * 10**6), VMEM_ROUND,
    )(landing, incoming, remote_weights, mixed, recip, first)


def on_device(target_sums, counts, band_offsets, band_weights, send_tiles, landing_tiles, remote_weights):
    count_tiles, _, width, _ = band_weights.shape
    shards = remote_weights.shape[0]
    reach = count_tiles // 2
    counts = counts.reshape(count_tiles, width)
    send, landing, offsets = send_tiles.reshape(-1), landing_tiles.reshape(-1), band_offsets.reshape(-1)
    parity = lax.axis_index("item") % 2
    odd = parity.reshape(1)
    inner_pairs = [(i, i ^ 1) for i in range(shards)]
    outer_pairs = [(i, i + 1 if i % 2 else i - 1) for i in range(1, shards - 1)]

    def swap(inner, outer):
        return lax.ppermute(inner, "item", inner_pairs), lax.ppermute(outer, "item", outer_pairs)

    def exchange(inner, outer, block, *weights):
        halo = swap(inner, outer)
        outgoing = fill_messages(odd, send, inner, outer, block, *weights)
        incoming = lax.all_to_all(outgoing, "item", split_axis=0, concat_axis=0, tiled=True)
        return halo, incoming

    inner, outer, block = prep(odd, target_sums, counts, shards)
    halo, incoming = exchange(inner, outer, block, remote_weights)
    mixed, sums = band_product(True, odd, offsets, target_sums, counts, inner, outer, *halo, band_weights)
    below, above = sums[:reach], sums[reach + count_tiles :]
    from_inner, from_outer = swap(
        jnp.where(parity == 1, below, above), jnp.where(parity == 1, above, below)
    )
    lower, upper = (
        jnp.where(parity == 1, from_inner, from_outer), jnp.where(parity == 1, from_outer, from_inner)
    )
    columns = sums[reach : reach + count_tiles] + jnp.concatenate([lower, upper], axis=0)
    inner, outer, block, recip, first = first_round(
        odd, send, landing, incoming, remote_weights, mixed, columns
    )
    halo, incoming = exchange(inner, outer, block)
    (mixed,) = band_product(False, odd, offsets, target_sums, counts, inner, outer, *halo, band_weights)
    return last_round(landing, incoming, remote_weights, mixed, recip, first)


def solution(mesh):
    return jax.shard_map(
        on_device,
        mesh=mesh,
        in_specs=(
            P(None, "item"),
            P("item"),
            P("item", None),
            P("item", None, None, None),
            P("item", None),
            P("item", None),
            P("item", None, None),
        ),
        out_specs=P(None, "item"),
        check_vma=False,
    )
```
